128 devices in a mesh: row: 4 (over x_hi, core), col: 4 (over y), depth: 8 (over z, x_lo).
Axes of the slice: x: 4 (x_hi: 2, x_lo: 2; x = x_hi * 2 + x_lo), y: 4, z: 4, core: 2. Of those that a mesh axis runs over, the one named last changes fastest.
Arguments:
- tokens: bfloat16 [8192, 6144], P(('depth', 'col'), 'row'), may hold values from -6 to 6
- weight: bfloat16 [6144, 12288], P('row', 'col'), may hold values from -0.078125 to 0.078125
- cotangent: bfloat16 [8192, 12288], P(('depth', 'row'), 'col'), may hold values from -6 to 6
Outputs:
- activation: bfloat16 [8192, 12288], P(('depth', 'row'), 'col')
- input_grad: bfloat16 [8192, 6144], P(('depth', 'col'), 'row')
- weight_grad: bfloat16 [6144, 12288], P('row', ('col', 'depth'))
The draws below stay inside these ranges and needn't reach their ends.
All inputs are finite; a program needn't handle non-finite values.
Results may differ from the reference program's by a relative error of at most 0.02.
Values may be sent and summed in bfloat16 or wider, within the bound.
No kernel may reach another device: no remote copies, remote signals or barrier semaphores. Data moves between devices by JAX's collectives and lax.ppermute only.
A program may use at most 128 MiB of HBM per device.

```python
import jax
import jax.numpy as jnp
from jax import lax

D = 6144
FF = 12288
TOKENS = 8192
PANEL_D = 1536
PANEL_F = 3072
GROUP_TOK = 1024
N_ROW = 4
N_COL = 4
N_DEPTH = 8


def raised(result, rng, source, target, parts, factor):
    def block_of(position):
        return (jnp.arange(result.shape[position]) // (result.shape[position] // parts)).reshape((-1,) + (1,) * (result.ndim - 1 - position))

    first = jax.random.permutation(rng, parts)[block_of(target)]
    second = (block_of(target) + parts // 2) % parts
    return jnp.where((block_of(source) == first) | (block_of(source) == second), factor * result, result)


def block_levels(key, shape, pieces, smallest, high):
    factor_of = 1.0
    for position, parts in pieces:
        draws = jax.random.uniform(jax.random.fold_in(jax.random.fold_in(key, 6), position), (parts,), jnp.float32, smallest / len(pieces), high / len(pieces))
        factor_of = factor_of * jnp.repeat(jnp.exp(draws), shape[position] // parts).reshape((-1,) + (1,) * (len(shape) - 1 - position))
    return factor_of


def normal_values(key, shape, width, bound, shards=(), kind=jnp.bfloat16):
    level = block_levels(key, shape, shards, -0.22, 0.18) if shards else 1.0
    array = jax.random.normal(key, shape, jnp.float32) * width * level
    return jnp.minimum(jnp.maximum(array, -bound), bound).astype(kind)


def noise_with(own_key, dims, width, limit, cuts, heavy, kind=jnp.bfloat16):
    result = width * jax.random.normal(own_key, dims, jnp.float32)
    if cuts:
        result = result * block_levels(own_key, dims, cuts, -0.22, 0.18)
    return jnp.clip(raised(result, jax.random.fold_in(own_key, 3), *heavy), -limit, limit).astype(kind)


def setup_inputs(seed: int = 0) -> dict:
    key_list = jax.random.split(jax.random.key(seed), 4)
    tokens = normal_values(key_list[0], (TOKENS, D), 1.0, 6.0, ((0, 32), (1, 4)))
    weight = normal_values(key_list[1], (D, FF), D ** -0.5, 0.078125, ((0, 4), (1, 4)))
    cotangent = noise_with(key_list[2], (TOKENS, FF), 1.0, 6.0, ((0, 32), (1, 4)), (0, 1, 32, 2.75))
    return {"tokens": tokens, "weight": weight, "cotangent": cotangent}


gelu_coef = 0.7978845608028654


def rounded(value):
    return lax.optimization_barrier(value.astype(jnp.bfloat16)).astype(jnp.float32)


def reference(tokens, weight, cotangent):
    pre = jnp.zeros((TOKENS, FF), jnp.float32)
    for block in range(N_ROW):
        lower = block * PANEL_D
        pre = pre + rounded(jnp.dot(tokens[:, lower:lower + PANEL_D], weight[lower:lower + PANEL_D, :], preferred_element_type=jnp.float32))
    inner = gelu_coef * (pre + 0.044715 * pre * pre * pre)
    tangent = jnp.tanh(inner)
    activation = (0.5 * pre * (1.0 + tangent)).astype(jnp.bfloat16)
    slope = 0.5 * (1.0 + tangent) + 0.5 * pre * (1.0 - tangent * tangent) * gelu_coef * (1.0 + 3.0 * 0.044715 * pre * pre)
    pre_grad = (cotangent.astype(jnp.float32) * slope).astype(jnp.bfloat16)
    input_grad = jnp.zeros((TOKENS, D), jnp.float32)
    for block in range(N_COL):
        lower = block * PANEL_F
        term = lax.dot_general(pre_grad[:, lower:lower + PANEL_F], weight[:, lower:lower + PANEL_F], (((1,), (1,)), ((), ())), preferred_element_type=jnp.float32)
        input_grad = input_grad + rounded(term)
    weight_grad = jnp.zeros((D, FF), jnp.float32)
    for block in range(N_DEPTH):
        lower = block * GROUP_TOK
        term = lax.dot_general(tokens[lower:lower + GROUP_TOK, :], pre_grad[lower:lower + GROUP_TOK, :], (((0,), (0,)), ((), ())), preferred_element_type=jnp.float32)
        weight_grad = weight_grad + rounded(term)
    return activation, input_grad.astype(jnp.bfloat16), weight_grad.astype(jnp.bfloat16)
```

```python
import functools

import jax
import jax.numpy as jnp
from jax import lax
from jax.experimental import pallas as pl
from jax.experimental.pallas import tpu as pltpu
from jax.sharding import Mesh
from jax.sharding import PartitionSpec as P

K = 1536
F = 3072
S = 256
CHUNKS = 3
DEPTH = 8
CW = F // CHUNKS
HALF = CW // 2
LANE = 128
gelu_coef = 0.7978845608028654
bf16 = jnp.bfloat16
f32 = jnp.float32
MIB = 1 << 20


def params(mib):
    return pltpu.CompilerParams(vmem_limit_bytes=mib * MIB)


def cost(flops, bytes_accessed, transcendentals=0):
    return pl.CostEstimate(flops=flops, bytes_accessed=bytes_accessed, transcendentals=transcendentals)


def partial_kernel(q_ref, b0, b1, b2, b3, w_ref, send_ref, keep_ref, tk_ref, sems):
    @pl.when(pl.program_id(0) == 0)
    def _():
        q = q_ref[0]
        copies = []
        for m, block in enumerate((b0, b1, b2, b3)):
            slot = pl.multiple_of(jnp.bitwise_xor(q, m) * S, S)
            copies.append(pltpu.make_async_copy(block, tk_ref.at[pl.ds(slot, S)], sems.at[m]))
        for copy in copies:
            copy.start()
        for copy in copies:
            copy.wait()

    w = w_ref[...]
    for k, (ref, at) in ((1, (send_ref, 0)), (3, (send_ref, 1)), (0, (keep_ref, 0)), (2, (keep_ref, 1))):
        term = jnp.dot(tk_ref[k * S:(k + 1) * S, :], w, preferred_element_type=f32)
        ref[at * S:(at + 1) * S, :] = term.astype(bf16)


def block_partials(q, blocks, weight):
    tile = 512
    grid_spec = pltpu.PrefetchScalarGridSpec(
        num_scalar_prefetch=1,
        grid=(F // tile,),
        in_specs=[pl.BlockSpec(memory_space=pl.ANY)] * 4 + [pl.BlockSpec((K, tile), lambda i, q: (0, i))],
        out_specs=[
            pl.BlockSpec((2 * S, tile), lambda i, q: (0, i)),
            pl.BlockSpec((2 * S, tile), lambda i, q: (0, i)),
            pl.BlockSpec((4 * S, K), lambda i, q: (0, 0)),
        ],
        scratch_shapes=[pltpu.SemaphoreType.DMA((4,))],
    )
    return pl.pallas_call(
        partial_kernel,
        grid_spec=grid_spec,
        out_shape=[
            jax.ShapeDtypeStruct((2 * S, F), bf16),
            jax.ShapeDtypeStruct((2 * S, F), bf16),
            jax.ShapeDtypeStruct((4 * S, K), bf16),
        ],
        compiler_params=params(40),
        cost_estimate=cost(2 * 4 * S * K * F, 21 * MIB),
        name="block_partials",
    )(q, *blocks, weight)


def gelu_kernel(xl_ref, own_ref, core_ref, far_ref, cot_ref, act_ref, *outs):
    xl = xl_ref[0]
    pgs, halves = outs[:CHUNKS], outs[CHUNKS:]
    pieces = {}
    for d in range(DEPTH):
        for f in range(CHUNKS):
            at = slice((d * CHUNKS + f) * LANE, (d * CHUNKS + f + 1) * LANE)
            pre = own_ref[:, at].astype(f32) + core_ref[:, at].astype(f32) + far_ref[:, at].astype(f32)
            inner = gelu_coef * (pre + 0.044715 * pre * pre * pre)
            tangent = jnp.tanh(inner)
            act_ref[:, at] = (0.5 * pre * (1.0 + tangent)).astype(bf16)
            slope = 0.5 * (1.0 + tangent) + 0.5 * pre * (1.0 - tangent * tangent) * gelu_coef * (
                1.0 + 3.0 * 0.044715 * pre * pre
            )
            grad = (cot_ref[:, at].astype(f32) * slope).astype(bf16)
            pgs[f][:, d * LANE:(d + 1) * LANE] = grad
            pieces[f, d % 2] = grad
            if d % 2:
                z = d // 2
                halves[f][:, z * LANE:(z + 1) * LANE] = jnp.where(xl == 0, pieces[f, 1], pieces[f, 0])


def gelu_pair(xl, keep, core, far, cot):
    rows = 64
    grid_spec = pltpu.PrefetchScalarGridSpec(
        num_scalar_prefetch=1,
        grid=(S // rows,),
        in_specs=[pl.BlockSpec((rows, F), lambda i, x: (i, 0))] * 4,
        out_specs=[pl.BlockSpec((rows, F), lambda i, x: (i, 0))]
        + [pl.BlockSpec((rows, CW), lambda i, x: (i, 0))] * CHUNKS
        + [pl.BlockSpec((rows, HALF), lambda i, x: (i, 0))] * CHUNKS,
    )
    outs = pl.pallas_call(
        gelu_kernel,
        grid_spec=grid_spec,
        out_shape=[jax.ShapeDtypeStruct((S, F), bf16)]
        + [jax.ShapeDtypeStruct((S, CW), bf16)] * CHUNKS
        + [jax.ShapeDtypeStruct((S, HALF), bf16)] * CHUNKS,
        compiler_params=params(40),
        cost_estimate=cost(30 * S * F, 10 * MIB, S * F),
        name="gelu_pair",
    )(xl, keep, core, far, cot)
    return outs[0], outs[1:1 + CHUNKS], outs[1 + CHUNKS:]


def weight_kernel(ids_ref, tk_ref, tx_ref, *refs):
    own, other, out_ref, pg = refs[:4], refs[4:8], refs[8], refs[9]

    @pl.when(pl.program_id(0) == 0)
    def _():
        xl, r = ids_ref[0], ids_ref[1]
        for k in range(4):
            for z in range(4):
                at = pl.multiple_of((2 * z + xl) * LANE, LANE)
                pg[k * S:(k + 1) * S, z * LANE:(z + 1) * LANE] = own[k][:, pl.ds(at, LANE)]
            slot = pl.multiple_of(4 * S + jnp.bitwise_xor(r, k) * S, S)
            pg[pl.ds(slot, S), :] = other[k][...]

    total = jnp.dot(tk_ref[...], pg[:4 * S, :], preferred_element_type=f32)
    total += jnp.dot(tx_ref[...], pg[4 * S:, :], preferred_element_type=f32)
    for z in range(4):
        out_ref[z] = total[:, z * LANE:(z + 1) * LANE].astype(bf16)


def weight_part(ids, tk, tx, own, other):
    rows = 512
    grid_spec = pltpu.PrefetchScalarGridSpec(
        num_scalar_prefetch=1,
        grid=(K // rows,),
        in_specs=[pl.BlockSpec((rows, 4 * S), lambda i, x: (i, 0))] * 2
        + [pl.BlockSpec((S, CW), lambda i, x: (0, 0))] * 4
        + [pl.BlockSpec((S, HALF), lambda i, x: (0, 0))] * 4,
        out_specs=pl.BlockSpec((4, rows, LANE), lambda i, x: (0, i, 0)),
        scratch_shapes=[pltpu.VMEM((8 * S, HALF), bf16)],
    )
    return pl.pallas_call(
        weight_kernel,
        grid_spec=grid_spec,
        out_shape=jax.ShapeDtypeStruct((4, K, LANE), bf16),
        compiler_params=params(40),
        cost_estimate=cost(2 * 8 * S * K * HALF, 11 * MIB),
        name="weight_part",
    )(ids, tk, tx, *own, *other)


def input_kernel(q_ref, *refs):
    grads, w_ref, outs, lhs, sems = refs[:12], refs[12], refs[13:17], refs[17], refs[18]

    @pl.when(pl.program_id(0) == 0)
    def _():
        q = q_ref[0]
        copies = []
        for k in range(4):
            slot = pl.multiple_of(jnp.bitwise_xor(q, k) * S, S)
            for f in range(CHUNKS):
                copies.append(
                    pltpu.make_async_copy(
                        grads[k * CHUNKS + f],
                        lhs.at[pl.ds(slot, S), pl.ds(f * CW, CW)],
                        sems.at[k * CHUNKS + f],
                    )
                )
        for copy in copies:
            copy.start()
        for copy in copies:
            copy.wait()

    w = w_ref[...]
    for m in range(4):
        outs[m][...] = jnp.dot(lhs[m * S:(m + 1) * S, :], w, preferred_element_type=f32).astype(bf16)


def input_part(q, grads, weight_t):
    tile = 512
    grid_spec = pltpu.PrefetchScalarGridSpec(
        num_scalar_prefetch=1,
        grid=(K // tile,),
        in_specs=[pl.BlockSpec(memory_space=pl.ANY)] * 12 + [pl.BlockSpec((F, tile), lambda i, q: (0, i))],
        out_specs=[pl.BlockSpec((S, tile), lambda i, q: (0, i))] * 4,
        scratch_shapes=[pltpu.VMEM((4 * S, F), bf16), pltpu.SemaphoreType.DMA((12,))],
    )
    return pl.pallas_call(
        input_kernel,
        grid_spec=grid_spec,
        out_shape=[jax.ShapeDtypeStruct((S, K), bf16)] * 4,
        compiler_params=params(40),
        cost_estimate=cost(2 * 4 * S * K * F, 18 * MIB),
        name="input_part",
    )(q, *grads, weight_t)


def swap(value, axis, mask):
    n = lax.axis_size(axis)
    return lax.ppermute(value, axis, [(i, i ^ mask) for i in range(n)])


def shards(tokens, weight, cotangent):
    xh, core, y, xl = (lax.axis_index(a) for a in ("xh", "core", "y", "xl"))
    r = 2 * xh + core
    q = jnp.bitwise_xor(r, y).astype(jnp.int32).reshape(1)
    ids = jnp.stack([xl, r]).astype(jnp.int32)

    blocks = [tokens] + [swap(tokens, "y", m) for m in (1, 2, 3)]
    other_tokens = lax.all_gather(swap(tokens, "xl", 1), "y", axis=0, tiled=True)
    weight_t = weight.reshape(K, DEPTH, CHUNKS, LANE).transpose(2, 1, 3, 0).reshape(F, K)

    send, keep, tk = block_partials(q, blocks, weight)
    came = swap(send, "core", 1)
    second = (keep[S:].astype(f32) + came[S:].astype(f32)).astype(bf16)
    far = swap(second, "xh", 1)
    activation, grads, halves = gelu_pair(ids[:1], keep, came, far, cotangent)

    tk_t = tk.T
    tx_t = other_tokens.T
    own = []
    sums = []
    for f in range(CHUNKS):
        pair = swap(grads[f], "xh", 1)
        own.append([grads[f], swap(grads[f], "core", 1), pair, swap(pair, "core", 1)])
        near = swap(halves[f], "xl", 1)
        cross = lax.ppermute(halves[f], ("xh", "xl"), [(i, 3 - i) for i in range(4)])
        other = [near, swap(near, "core", 1), cross, swap(cross, "core", 1)]
        part = weight_part(ids, tk_t, tx_t, own[f], other)
        sums.append(lax.psum_scatter(part, "z", scatter_dimension=0, tiled=True)[0])
    weight_grad = jnp.concatenate(sums, axis=1)

    dx = input_part(q, [own[f][k] for k in range(4) for f in range(CHUNKS)], weight_t)
    total = dx[0].astype(f32)
    for m in (1, 2, 3):
        total += swap(dx[m], "y", m).astype(f32)
    return activation, total.astype(bf16), weight_grad


def solution(mesh):
    split = Mesh(mesh.devices.reshape(2, 2, 4, 4, 2), ("xh", "core", "y", "z", "xl"))
    hidden = P(("z", "xl", "xh", "core"), "y")
    tokens = P(("z", "xl", "y"), ("xh", "core"))
    return jax.shard_map(
        shards,
        mesh=split,
        in_specs=(tokens, P(("xh", "core"), "y"), hidden),
        out_specs=(hidden, tokens, P(("xh", "core"), ("y", "z", "xl"))),
        check_vma=False,
    )
```

```python
import jax
import jax.numpy as jnp
from jax import lax
from jax.experimental import pallas as pl
from jax.experimental.pallas import tpu as pltpu
from jax.sharding import Mesh
from jax.sharding import PartitionSpec as P

K = 1536
F = 3072
S = 256
H = 128
CHUNKS = 3
DEPTH = 8
CW = F // CHUNKS
HALF = CW // 2
LANE = 128
gelu_coef = 0.7978845608028654
bf16 = jnp.bfloat16
f32 = jnp.float32
MIB = 1 << 20
ANY = pl.BlockSpec(memory_space=pl.ANY)


def params():
    return pltpu.CompilerParams(vmem_limit_bytes=60 * MIB)


def cost(flops, bytes_accessed, transcendentals=0):
    return pl.CostEstimate(flops=flops, bytes_accessed=bytes_accessed, transcendentals=transcendentals)


def after_kernel(*refs):
    pass


def after(value, *others):
    return pl.pallas_call(
        after_kernel,
        in_specs=[ANY] * (1 + len(others)),
        out_specs=ANY,
        out_shape=jax.ShapeDtypeStruct(value.shape, value.dtype),
        input_output_aliases={0: 0},
        cost_estimate=cost(0, 0),
        name="after",
    )(value, *others)


def partial_kernel(q_ref, b0, b1, b2, b3, w_ref, p0_ref, p1_ref, p2_ref, p3_ref, tk_ref, sems):
    @pl.when(pl.program_id(0) == 0)
    def _():
        q = q_ref[0]
        copies = []
        for m, block in enumerate((b0, b1, b2, b3)):
            slot = pl.multiple_of(jnp.bitwise_xor(q, m) * H, H)
            copies.append(pltpu.make_async_copy(block, tk_ref.at[pl.ds(slot, H)], sems.at[m]))
        for copy in copies:
            copy.start()
        for copy in copies:
            copy.wait()

    term = jnp.dot(tk_ref[...], w_ref[...], preferred_element_type=f32).astype(bf16)
    for k, ref in enumerate((p0_ref, p1_ref, p2_ref, p3_ref)):
        ref[...] = term[k * H:(k + 1) * H, :]


def block_partials(q, blocks, weight):
    tile = 512
    grid_spec = pltpu.PrefetchScalarGridSpec(
        num_scalar_prefetch=1,
        grid=(F // tile,),
        in_specs=[ANY] * 4 + [pl.BlockSpec((K, tile), lambda i, q: (0, i))],
        out_specs=[pl.BlockSpec((H, tile), lambda i, q: (0, i))] * 4 + [pl.BlockSpec((4 * H, K), lambda i, q: (0, 0))],
        scratch_shapes=[pltpu.SemaphoreType.DMA((4,))],
    )
    return pl.pallas_call(
        partial_kernel,
        grid_spec=grid_spec,
        out_shape=[jax.ShapeDtypeStruct((H, F), bf16)] * 4 + [jax.ShapeDtypeStruct((4 * H, K), bf16)],
        compiler_params=params(),
        cost_estimate=cost(2 * 4 * H * K * F, 16 * MIB),
        name="block_partials",
    )(q, *blocks, weight)


def gelu_kernel(xl_ref, own_ref, core_ref, far_ref, cot_ref, *refs):
    outs = refs[-(1 + 2 * CHUNKS):]
    xl = xl_ref[0]
    act_ref, pgs, halves = outs[0], outs[1:1 + CHUNKS], outs[1 + CHUNKS:]
    pieces = {}
    for d in range(DEPTH):
        for f in range(CHUNKS):
            at = slice((d * CHUNKS + f) * LANE, (d * CHUNKS + f + 1) * LANE)
            pre = own_ref[:, at].astype(f32) + core_ref[:, at].astype(f32) + far_ref[:, at].astype(f32)
            inner = gelu_coef * (pre + 0.044715 * pre * pre * pre)
            tangent = jnp.tanh(inner)
            act_ref[:, at] = (0.5 * pre * (1.0 + tangent)).astype(bf16)
            slope = 0.5 * (1.0 + tangent) + 0.5 * pre * (1.0 - tangent * tangent) * gelu_coef * (
                1.0 + 3.0 * 0.044715 * pre * pre
            )
            grad = (cot_ref[:, at].astype(f32) * slope).astype(bf16)
            pgs[f][:, d * LANE:(d + 1) * LANE] = grad
            pieces[f, d % 2] = grad
            if d % 2:
                z = d // 2
                halves[f][:, z * LANE:(z + 1) * LANE] = jnp.where(xl == 0, pieces[f, 1], pieces[f, 0])


def gelu_pair(xl, own, core, far, cot, part, earlier=()):
    rows = 64
    steps = H // rows
    grid_spec = pltpu.PrefetchScalarGridSpec(
        num_scalar_prefetch=1,
        grid=(steps,),
        in_specs=[pl.BlockSpec((rows, F), lambda i, x: (i, 0))] * 3
        + [pl.BlockSpec((rows, F), lambda i, x: (i + part * steps, 0))]
        + [ANY] * len(earlier),
        out_specs=[pl.BlockSpec((rows, F), lambda i, x: (i + part * steps, 0))]
        + [pl.BlockSpec((rows, CW), lambda i, x: (i + part * steps, 0))] * CHUNKS
        + [pl.BlockSpec((rows, HALF), lambda i, x: (i + part * steps, 0))] * CHUNKS,
    )
    return pl.pallas_call(
        gelu_kernel,
        grid_spec=grid_spec,
        out_shape=[jax.ShapeDtypeStruct((S, F), bf16)]
        + [jax.ShapeDtypeStruct((S, CW), bf16)] * CHUNKS
        + [jax.ShapeDtypeStruct((S, HALF), bf16)] * CHUNKS,
        input_output_aliases={5 + i: i for i in range(len(earlier))},
        compiler_params=params(),
        cost_estimate=cost(30 * H * F, 5 * MIB, H * F),
        name="gelu_pair",
    )(xl, own, core, far, cot, *earlier)


def weight_kernel(ids_ref, ta_ref, tb_ref, tx_ref, *refs):
    own, other, out_ref, pg = refs[:4], refs[4:8], refs[8], refs[9]

    @pl.when(pl.program_id(0) == 0)
    def _():
        xl, r = ids_ref[0], ids_ref[1]
        for k in range(4):
            for z in range(4):
                at = pl.multiple_of((2 * z + xl) * LANE, LANE)
                for part in range(2):
                    row = (4 * part + k) * H
                    pg[row:row + H, z * LANE:(z + 1) * LANE] = own[k][part * H:(part + 1) * H, pl.ds(at, LANE)]
            slot = pl.multiple_of(4 * S + jnp.bitwise_xor(r, k) * S, S)
            pg[pl.ds(slot, S), :] = other[k][...]

    total = jnp.dot(ta_ref[...], pg[:4 * H, :], preferred_element_type=f32)
    total += jnp.dot(tb_ref[...], pg[4 * H:8 * H, :], preferred_element_type=f32)
    total += jnp.dot(tx_ref[...], pg[8 * H:, :], preferred_element_type=f32)
    for z in range(4):
        out_ref[z] = total[:, z * LANE:(z + 1) * LANE].astype(bf16)


def weight_part(ids, ta, tb, tx, own, other):
    rows = 512
    grid_spec = pltpu.PrefetchScalarGridSpec(
        num_scalar_prefetch=1,
        grid=(K // rows,),
        in_specs=[pl.BlockSpec((rows, 4 * H), lambda i, x: (i, 0))] * 2
        + [pl.BlockSpec((rows, 4 * S), lambda i, x: (i, 0))]
        + [pl.BlockSpec((S, CW), lambda i, x: (0, 0))] * 4
        + [pl.BlockSpec((S, HALF), lambda i, x: (0, 0))] * 4,
        out_specs=pl.BlockSpec((4, rows, LANE), lambda i, x: (0, i, 0)),
        scratch_shapes=[pltpu.VMEM((8 * S, HALF), bf16)],
    )
    return pl.pallas_call(
        weight_kernel,
        grid_spec=grid_spec,
        out_shape=jax.ShapeDtypeStruct((4, K, LANE), bf16),
        compiler_params=params(),
        cost_estimate=cost(2 * 8 * S * K * HALF, 11 * MIB),
        name="weight_part",
    )(ids, ta, tb, tx, *own, *other)


def input_kernel(q_ref, *refs):
    grads, w_ref, outs, lhs, sems = refs[:12], refs[12], refs[13:17], refs[17], refs[18]

    @pl.when(pl.program_id(0) == 0)
    def _():
        q = q_ref[0]
        copies = []
        for k in range(4):
            slot = pl.multiple_of(jnp.bitwise_xor(q, k) * S, S)
            for f in range(CHUNKS):
                copies.append(
                    pltpu.make_async_copy(
                        grads[k * CHUNKS + f],
                        lhs.at[pl.ds(slot, S), pl.ds(f * CW, CW)],
                        sems.at[k * CHUNKS + f],
                    )
                )
        for copy in copies:
            copy.start()
        for copy in copies:
            copy.wait()

    w = jnp.concatenate(
        [
            w_ref[:, (d * CHUNKS + f) * LANE:(d * CHUNKS + f + 1) * LANE]
            for f in range(CHUNKS)
            for d in range(DEPTH)
        ],
        axis=1,
    )
    total = lax.dot_general(lhs[...], w, (((1,), (1,)), ((), ())), preferred_element_type=f32).astype(bf16)
    for m in range(4):
        outs[m][...] = total[m * S:(m + 1) * S, :]


def input_part(q, grads, weight):
    tile = 256
    grid_spec = pltpu.PrefetchScalarGridSpec(
        num_scalar_prefetch=1,
        grid=(K // tile,),
        in_specs=[ANY] * 12 + [pl.BlockSpec((tile, F), lambda i, q: (i, 0))],
        out_specs=[pl.BlockSpec((S, tile), lambda i, q: (0, i))] * 4,
        scratch_shapes=[pltpu.VMEM((4 * S, F), bf16), pltpu.SemaphoreType.DMA((12,))],
    )
    return pl.pallas_call(
        input_kernel,
        grid_spec=grid_spec,
        out_shape=[jax.ShapeDtypeStruct((S, K), bf16)] * 4,
        compiler_params=params(),
        cost_estimate=cost(2 * 4 * S * K * F, 18 * MIB),
        name="input_part",
    )(q, *grads, weight)


def swap(value, axis, mask):
    n = lax.axis_size(axis)
    return lax.ppermute(value, axis, [(i, i ^ mask) for i in range(n)])


def shards(tokens, weight, cotangent):
    xh, core, y, xl, z = (lax.axis_index(a) for a in ("xh", "core", "y", "xl", "z"))
    r = 2 * xh + core
    q = jnp.bitwise_xor(r, y).astype(jnp.int32).reshape(1)
    ids = jnp.stack([xl, r]).astype(jnp.int32)

    parts = [tokens[:H], tokens[H:]]
    others = lax.all_gather(swap(tokens, "xl", 1), "y", axis=0, tiled=True)
    tx = others.T
    out = ()
    turned = []
    gathered = None
    for part in range(2):
        mine = parts[part] if part == 0 else after(parts[part], gathered[2])
        gathered = [swap(mine, "y", 2), swap(mine, "y", 1), swap(mine, "y", 3)]
        p0, p1, p2, p3, tk = block_partials(q, [mine, gathered[1], gathered[0], gathered[2]], weight)
        second = (p2.astype(f32) + swap(p3, "core", 1).astype(f32)).astype(bf16)
        far = swap(second, "xh", 1)
        turned.append(tk.T)
        out = gelu_pair(ids[:1], p0, swap(p1, "core", 1), far, cotangent, part, out)
    activation, grads, halves = out[0], out[1:1 + CHUNKS], out[1 + CHUNKS:]

    own = []
    sums = []
    for f in range(CHUNKS):
        pair = swap(grads[f], "xh", 1)
        own.append([grads[f], swap(grads[f], "core", 1), pair, swap(pair, "core", 1)])
        near = swap(halves[f], "xl", 1)
        cross = lax.ppermute(halves[f], ("xh", "xl"), [(i, 3 - i) for i in range(4)])
        other = [near, swap(near, "core", 1), cross, swap(cross, "core", 1)]
        part = weight_part(ids, turned[0], turned[1], tx, own[f], other)
        if f == 0:
            sums.append(lax.psum_scatter(part, "z", scatter_dimension=0, tiled=True)[0].astype(f32))
        else:
            total = lax.dynamic_index_in_dim(part, z, 0, False).astype(f32)
            for m in (2, 1, 3):
                piece = lax.dynamic_index_in_dim(part, jnp.bitwise_xor(z, m), 0, False)
                total += swap(piece, "z", m).astype(f32)
            sums.append(total)
    weight_grad = jnp.concatenate(sums, axis=1).astype(bf16)

    dx = input_part(q, [own[f][k] for k in range(4) for f in range(CHUNKS)], weight)
    total = dx[0].astype(f32)
    for m in (2, 1, 3):
        total += swap(dx[m], "y", m).astype(f32)
    return activation, total.astype(bf16), weight_grad


def solution(mesh):
    split = Mesh(mesh.devices.reshape(2, 2, 4, 4, 2), ("xh", "core", "y", "z", "xl"))
    hidden = P(("z", "xl", "xh", "core"), "y")
    tokens = P(("z", "xl", "y"), ("xh", "core"))
    return jax.shard_map(
        shards,
        mesh=split,
        in_specs=(tokens, P(("xh", "core"), "y"), hidden),
        out_specs=(hidden, tokens, P(("xh", "core"), ("y", "z", "xl"))),
        check_vma=False,
    )
```

```python
import jax
import jax.numpy as jnp
from jax import lax
from jax.experimental import pallas as pl
from jax.experimental.pallas import tpu as pltpu
from jax.sharding import Mesh
from jax.sharding import PartitionSpec as P

K = 1536
F = 3072
S = 256
H = 128
DEPTH = 8
LANE = 128
UNITS = F // (DEPTH * LANE)
CHUNKS = ((0, 2), (2, 1))
N = len(CHUNKS)
gelu_coef = 0.7978845608028654
bf16 = jnp.bfloat16
f32 = jnp.float32
MIB = 1 << 20
TF, TG, TK, TE = 0.01, 30, 3, 300
LATE = True
ANY = pl.BlockSpec(memory_space=pl.ANY)
PARAMS = pltpu.CompilerParams(vmem_limit_bytes=63 * MIB)


def cost(micros):
    return pl.CostEstimate(flops=int(micros * 1.15e9), bytes_accessed=int(micros * 3.6e6), transcendentals=0)


def width(chunk):
    return DEPTH * CHUNKS[chunk][1] * LANE


def after_kernel(*refs):
    pass


def after(values, other, micros=300):
    return pl.pallas_call(
        after_kernel,
        in_specs=[ANY] * (len(values) + 1),
        out_specs=[ANY] * len(values),
        out_shape=[jax.ShapeDtypeStruct(value.shape, value.dtype) for value in values],
        input_output_aliases={n: n for n in range(len(values))},
        cost_estimate=cost(micros),
        name="after",
    )(*values, other)


def partial_kernel(q_ref, b0, b1, b2, b3, w_ref, *refs):
    p0_ref, p1_ref, p2_ref, p3_ref, tk_ref = refs[-5:]

    @pl.when(pl.program_id(0) == 0)
    def _():
        q = q_ref[0]
        for m, block in enumerate((b0, b1, b2, b3)):
            slot = pl.multiple_of(jnp.bitwise_xor(q, m) * H, H)
            tk_ref[pl.ds(slot, H), :] = block[...]

    term = jnp.dot(tk_ref[...], w_ref[...], preferred_element_type=f32).astype(bf16)
    for k, ref in enumerate((p0_ref, p1_ref, p2_ref, p3_ref)):
        ref[...] = term[k * H:(k + 1) * H, :]


def block_partials(q, blocks, weight, part, earlier, wait):
    tile = 1024
    rows = [pl.BlockSpec((H, K), lambda i, q, at=part if block.shape[0] == S else 0: (at, 0)) for block in blocks]
    grid_spec = pltpu.PrefetchScalarGridSpec(
        num_scalar_prefetch=1,
        grid=(F // tile,),
        in_specs=rows + [pl.BlockSpec((K, tile), lambda i, q: (0, i))] + [ANY] * (len(earlier) + len(wait)),
        out_specs=[pl.BlockSpec((H, tile), lambda i, q: (0, i))] * 4
        + [pl.BlockSpec((4 * H, K), lambda i, q: (part, 0))],
    )
    return pl.pallas_call(
        partial_kernel,
        grid_spec=grid_spec,
        out_shape=[jax.ShapeDtypeStruct((H, F), bf16)] * 4 + [jax.ShapeDtypeStruct((4 * S, K), bf16)],
        input_output_aliases={6: 4} if earlier else {},
        compiler_params=PARAMS,
        cost_estimate=cost(TF),
        name="block_partials",
    )(q, *blocks, weight, *earlier, *wait)


def gelu_kernel(n_pg, xl_ref, own_ref, core_ref, far_ref, cot_ref, *refs):
    outs = refs[-(1 + n_pg + N):]
    xl = xl_ref[0]
    act_ref, pgs, halves = outs[0], outs[1 + N:], outs[1:1 + N]
    base = 0
    for chunk, (start, units) in enumerate(CHUNKS):
        size = units * LANE
        pieces = []
        for d in range(DEPTH):
            at = slice(d * UNITS * LANE + start * LANE, d * UNITS * LANE + start * LANE + size)
            pre = own_ref[:, at].astype(f32) + core_ref[:, at].astype(f32) + far_ref[:, at].astype(f32)
            inner = gelu_coef * (pre + 0.044715 * pre * pre * pre)
            tangent = jnp.tanh(inner)
            act_ref[:, at] = (0.5 * pre * (1.0 + tangent)).astype(bf16)
            slope = 0.5 * (1.0 + tangent) + 0.5 * pre * (1.0 - tangent * tangent) * gelu_coef * (
                1.0 + 3.0 * 0.044715 * pre * pre
            )
            grad = (cot_ref[:, at].astype(f32) * slope).astype(bf16)
            if n_pg == 1:
                pgs[0][:, base + d * size:base + (d + 1) * size] = grad
            else:
                pgs[chunk][:, d * size:(d + 1) * size] = grad
            pieces.append(grad)
            if d % 2:
                z = d // 2
                halves[chunk][:, z * size:(z + 1) * size] = jnp.where(xl == 0, pieces[d], pieces[d - 1])
        base += DEPTH * size


def gelu_pair(xl, own, core, far, cot, part, earlier, wait):
    rows = 64
    steps = H // rows
    widths = [width(chunk) for chunk in range(N)] if part else [F]
    whole = lambda w: pl.BlockSpec((rows, w), lambda i, x: (i + part * steps, 0))
    local = lambda w: pl.BlockSpec((rows, w), lambda i, x: (i, 0))
    grid_spec = pltpu.PrefetchScalarGridSpec(
        num_scalar_prefetch=1,
        grid=(steps,),
        in_specs=[local(F)] * 3 + [whole(F)] + [ANY] * (len(earlier) + len(wait)),
        out_specs=[whole(F)] + [whole(width(chunk) // 2) for chunk in range(N)] + [local(w) for w in widths],
    )
    outs = pl.pallas_call(
        lambda *refs: gelu_kernel(len(widths), *refs),
        grid_spec=grid_spec,
        out_shape=[jax.ShapeDtypeStruct((S, F), bf16)]
        + [jax.ShapeDtypeStruct((S, width(chunk) // 2), bf16) for chunk in range(N)]
        + [jax.ShapeDtypeStruct((H, w), bf16) for w in widths],
        input_output_aliases={5 + i: i for i in range(len(earlier))},
        compiler_params=PARAMS,
        cost_estimate=cost(TG),
        name="gelu_pair",
    )(xl, own, core, far, cot, *earlier, *wait)
    return outs[:1 + N], outs[1 + N:]


def weight_kernel(size, ids_ref, tk_ref, tx_ref, *refs):
    first, second, other = refs[:4], refs[4:8], refs[8:12]
    out_ref, pg = refs[-2:]

    @pl.when(pl.program_id(0) == 0)
    def _():
        xl, r = ids_ref[0], ids_ref[1]
        for k in range(4):
            for z in range(4):
                at = pl.multiple_of((2 * z + xl) * size, size)
                for part, grads in enumerate((first, second)):
                    row = (4 * part + k) * H
                    pg[row:row + H, z * size:(z + 1) * size] = grads[k][:, pl.ds(at, size)]
            slot = pl.multiple_of(4 * S + jnp.bitwise_xor(r, k) * S, S)
            pg[pl.ds(slot, S), :] = other[k][...]

    tokens = jnp.concatenate([tk_ref[...], tx_ref[...]], axis=0)
    total = lax.dot_general(tokens, pg[...], (((0,), (0,)), ((), ())), preferred_element_type=f32).astype(bf16)
    for z in range(4):
        out_ref[z] = total[:, z * size:(z + 1) * size]


def weight_part(ids, tk, tx, first, second, other, chunk, wait):
    rows = 512
    w = width(chunk)
    size = CHUNKS[chunk][1] * LANE
    before = sum(width(c) for c in range(chunk))
    assert before % w == 0
    grid_spec = pltpu.PrefetchScalarGridSpec(
        num_scalar_prefetch=1,
        grid=(K // rows,),
        in_specs=[pl.BlockSpec((4 * S, rows), lambda i, x: (0, i))] * 2
        + [pl.BlockSpec((H, w), lambda i, x: (0, before // w))] * 4
        + [pl.BlockSpec((H, w), lambda i, x: (0, 0))] * 4
        + [pl.BlockSpec((S, w // 2), lambda i, x: (0, 0))] * 4
        + [ANY] * len(wait),
        out_specs=pl.BlockSpec((4, rows, size), lambda i, x: (0, i, 0)),
        scratch_shapes=[pltpu.VMEM((8 * S, w // 2), bf16)],
    )
    return pl.pallas_call(
        lambda *refs: weight_kernel(size, *refs),
        grid_spec=grid_spec,
        out_shape=jax.ShapeDtypeStruct((4, K, size), bf16),
        compiler_params=PARAMS,
        cost_estimate=cost(TK),
        name="weight_part",
    )(ids, tk, tx, *first, *second, *other, *wait)


def input_kernel(pieces, r_ref, *refs):
    grads, w_ref, out_ref = refs[:4 * pieces], refs[4 * pieces], refs[-1]
    rows = [jnp.concatenate([grads[k * pieces + f][...] for f in range(pieces)], axis=1) for k in range(4)]
    w = jnp.concatenate(
        [
            w_ref[:, (d * UNITS + start) * LANE:(d * UNITS + start + units) * LANE]
            for start, units in CHUNKS
            for d in range(DEPTH)
        ],
        axis=1,
    )
    lhs = jnp.concatenate(rows, axis=0)
    total = lax.dot_general(lhs, w, (((1,), (1,)), ((), ())), preferred_element_type=f32).astype(bf16)
    for k in range(4):
        slot = pl.multiple_of(jnp.bitwise_xor(r_ref[1], k) * H, H)
        out_ref[pl.ds(slot, H), :] = total[k * H:(k + 1) * H, :]


def input_part(ids, grads, weight, wait):
    tile = 512
    grid_spec = pltpu.PrefetchScalarGridSpec(
        num_scalar_prefetch=1,
        grid=(K // tile,),
        in_specs=[pl.BlockSpec(grad.shape, lambda i, q: (0, 0)) for grad in grads]
        + [pl.BlockSpec((tile, F), lambda i, q: (i, 0))]
        + [ANY] * len(wait),
        out_specs=pl.BlockSpec((4 * H, tile), lambda i, q: (0, i)),
    )
    return pl.pallas_call(
        lambda *refs: input_kernel(len(grads) // 4, *refs),
        grid_spec=grid_spec,
        out_shape=jax.ShapeDtypeStruct((4 * H, K), bf16),
        compiler_params=PARAMS,
        cost_estimate=cost(TK),
        name="input_part",
    )(ids, *grads, weight, *wait)


def add_kernel(a_ref, b_ref, wait_ref, out_ref):
    out_ref[...] = (a_ref[...].astype(f32) + b_ref[...].astype(f32)).astype(bf16)


def add(a, b, wait):
    block = pl.BlockSpec((H, F // 2), lambda i: (0, i))
    return pl.pallas_call(
        add_kernel,
        grid=(2,),
        in_specs=[block, block, ANY],
        out_specs=block,
        out_shape=jax.ShapeDtypeStruct(a.shape, bf16),
        compiler_params=PARAMS,
        cost_estimate=cost(1),
        name="add",
    )(a, b, wait)


def fold_kernel(in_ref, *refs):
    total = in_ref[0].astype(f32)
    for n in range(1, in_ref.shape[0]):
        total += in_ref[n].astype(f32)
    refs[-1][...] = total.astype(bf16)


def fold(pieces, shape, at, earlier=()):
    block = pieces.shape[1:]
    return pl.pallas_call(
        fold_kernel,
        grid=(1,),
        in_specs=[pl.BlockSpec(pieces.shape, lambda i: (0, 0, 0))] + [ANY] * len(earlier),
        out_specs=pl.BlockSpec(block, lambda i: at),
        out_shape=jax.ShapeDtypeStruct(shape, bf16),
        input_output_aliases={1: 0} if earlier else {},
        compiler_params=PARAMS,
        cost_estimate=cost(TK),
        name="fold",
    )(pieces, *earlier)


def swap(value, axis, mask):
    n = lax.axis_size(axis)
    return lax.ppermute(value, axis, [(i, i ^ mask) for i in range(n)])


def shards(tokens, weight, cotangent):
    xh, core, y, xl, z = (lax.axis_index(a) for a in ("xh", "core", "y", "xl", "z"))
    r = 2 * xh + core
    q = jnp.bitwise_xor(r, y).astype(jnp.int32).reshape(1)
    ids = jnp.stack([xl, r]).astype(jnp.int32)

    partner = swap(tokens, "xl", 1)
    tx = lax.all_gather(partner, "y", axis=0, tiled=True)
    opposite = [swap(tokens[:H], "y", 2)]
    y1, y3 = swap(tokens, "y", 1), swap(tokens, "y", 3)
    opposite += after([swap(tokens[H:], "y", 2)], partner, TE)
    tk = ()
    wait = partner
    terms = []
    for part in range(2):
        p0, p1, p2, p3, *tk = block_partials(q, [tokens, y1, opposite[part], y3], weight, part, tk, (wait,))
        terms.append((p0, swap(p1, "core", 1)))
        if part == 0:
            wait = total = add(p2, swap(p3, "core", 1), opposite[1])
        else:
            shared, (first,) = gelu_pair(ids, *terms[0], swap(total, "xh", 1), cotangent, 0, (), ())
            total = add(p2, swap(p3, "core", 1), first if LATE else wait)
            terms[1] += (swap(total, "xh", 1),)
    first_far = swap(first, "xh", 1)
    (activation, *halves), second = gelu_pair(ids, *terms[1], cotangent, 1, shared, (tx,))
    far = [swap(value, "xh", 1) for value in second]
    near = [swap(half, "xl", 1) for half in halves]
    cross = [lax.ppermute(half, ("xh", "xl"), [(i, 3 - i) for i in range(4)]) for half in halves]

    def both(values, other):
        values = after(values, other)
        return [(value, swap(value, "core", 1)) for value in values]

    first, first_far = both([first, first_far], halves[0])
    first = [*first, *first_far]
    dxa = input_part(ids, first, weight, ())
    mine, theirs, n, c = both([second[0], far[0], near[0], cross[0]], dxa)
    grads = [[*mine, *theirs]]
    dw0 = weight_part(ids, tk[0], tx, first, grads[0], [*n, *c], 0, ())
    mine, theirs = both([second[1], far[1]], dw0)
    grads.append([*mine, *theirs])
    dxb = input_part(ids, [grads[g][k] for k in range(4) for g in range(N)], weight, ())

    dxb_own = dxb
    dxa, dxb = (lax.all_to_all(v.reshape(4, H, K), "y", 0, 0, tiled=True) for v in (dxa, dxb))
    input_grad = fold(dxa, (S, K), (0, 0))
    n, c = both([near[1], cross[1]], dxb_own)
    dw1 = weight_part(ids, tk[0], tx, first, grads[1], [*n, *c], 1, (input_grad,))

    dw0 = lax.psum_scatter(dw0, "z", scatter_dimension=0, tiled=True)[0]
    total = lax.dynamic_index_in_dim(dw1, z, 0, False).astype(f32)
    for m in (2, 1, 3):
        piece = lax.dynamic_index_in_dim(dw1, jnp.bitwise_xor(z, m), 0, False)
        total += swap(piece, "z", m).astype(f32)
    input_grad = fold(dxb, (S, K), (1, 0), (input_grad,))
    weight_grad = jnp.concatenate([dw0, total.astype(bf16)], axis=1)
    return activation, input_grad, weight_grad


def solution(mesh):
    split = Mesh(mesh.devices.reshape(2, 2, 4, 4, 2), ("xh", "core", "y", "z", "xl"))
    hidden = P(("z", "xl", "xh", "core"), "y")
    tokens = P(("z", "xl", "y"), ("xh", "core"))
    return jax.shard_map(
        shards,
        mesh=split,
        in_specs=(tokens, P(("xh", "core"), "y"), hidden),
        out_specs=(hidden, tokens, P(("xh", "core"), ("y", "z", "xl"))),
        check_vma=False,
    )
```

```python
import jax
import jax.numpy as jnp
from jax import lax
from jax.experimental import pallas as pl
from jax.experimental.pallas import tpu as pltpu
from jax.sharding import Mesh
from jax.sharding import PartitionSpec as P

K = 1536
F = 3072
S = 256
H = 128
DEPTH = 8
LANE = 128
UNITS = F // (DEPTH * LANE)
CHUNKS = ((0, 1), (1, 2))
N = len(CHUNKS)
LAID = (1, 0)
gelu_coef = 0.7978845608028654
bf16 = jnp.bfloat16
f32 = jnp.float32
MIB = 1 << 20
TF, TG, TK, TE, T4, T5 = 0.01, 30, 0.5, 300, 300, 300
ANY = pl.BlockSpec(memory_space=pl.ANY)
PARAMS = pltpu.CompilerParams(vmem_limit_bytes=63 * MIB)


def cost(micros):
    return pl.CostEstimate(flops=int(micros * 1.15e9), bytes_accessed=int(micros * 3.6e6), transcendentals=0)


def width(chunk):
    return DEPTH * CHUNKS[chunk][1] * LANE


def place(chunk):
    return sum(width(other) for other in LAID[:LAID.index(chunk)])


def after_kernel(*refs):
    pass


def after(values, other, micros=300):
    return pl.pallas_call(
        after_kernel,
        in_specs=[ANY] * (len(values) + 1),
        out_specs=[ANY] * len(values),
        out_shape=[jax.ShapeDtypeStruct(value.shape, value.dtype) for value in values],
        input_output_aliases={n: n for n in range(len(values))},
        cost_estimate=cost(micros),
        name="after",
    )(*values, other)


def partial_kernel(q_ref, b0, b1, b2, b3, w_ref, *refs):
    p0_ref, p1_ref, p2_ref, p3_ref, tk_ref = refs[-5:]

    @pl.when(pl.program_id(0) == 0)
    def _():
        q = q_ref[0]
        for m, block in enumerate((b0, b1, b2, b3)):
            slot = pl.multiple_of(jnp.bitwise_xor(q, m) * H, H)
            tk_ref[pl.ds(slot, H), :] = block[...]

    term = jnp.dot(tk_ref[...], w_ref[...], preferred_element_type=f32).astype(bf16)
    for k, ref in enumerate((p0_ref, p1_ref, p2_ref, p3_ref)):
        ref[...] = term[k * H:(k + 1) * H, :]


def block_partials(q, blocks, weight, part, earlier, wait):
    tile = 1024
    rows = [pl.BlockSpec((H, K), lambda i, q, at=part if block.shape[0] == S else 0: (at, 0)) for block in blocks]
    grid_spec = pltpu.PrefetchScalarGridSpec(
        num_scalar_prefetch=1,
        grid=(F // tile,),
        in_specs=rows + [pl.BlockSpec((K, tile), lambda i, q: (0, i))] + [ANY] * (len(earlier) + len(wait)),
        out_specs=[pl.BlockSpec((H, tile), lambda i, q: (0, i))] * 4
        + [pl.BlockSpec((4 * H, K), lambda i, q: (part, 0))],
    )
    return pl.pallas_call(
        partial_kernel,
        grid_spec=grid_spec,
        out_shape=[jax.ShapeDtypeStruct((H, F), bf16)] * 4 + [jax.ShapeDtypeStruct((4 * S, K), bf16)],
        input_output_aliases={6: 4} if earlier else {},
        compiler_params=PARAMS,
        cost_estimate=cost(TF),
        name="block_partials",
    )(q, *blocks, weight, *earlier, *wait)


def gelu_kernel(part, xl_ref, own_ref, core_ref, far_ref, cot_ref, *refs):
    act_ref, *outs = refs[-(2 + N + part * N):]
    halves, grad_ref, pieces = outs[:N], outs[N], outs[N + 1:]
    xl = xl_ref[0]
    for chunk, (start, units) in enumerate(CHUNKS):
        size = units * LANE
        base = place(chunk)
        for d in range(DEPTH):
            at = slice(d * UNITS * LANE + start * LANE, d * UNITS * LANE + start * LANE + size)
            pre = own_ref[:, at].astype(f32) + core_ref[:, at].astype(f32) + far_ref[:, at].astype(f32)
            inner = gelu_coef * (pre + 0.044715 * pre * pre * pre)
            tangent = jnp.tanh(inner)
            act_ref[:, at] = (0.5 * pre * (1.0 + tangent)).astype(bf16)
            slope = 0.5 * (1.0 + tangent) + 0.5 * pre * (1.0 - tangent * tangent) * gelu_coef * (
                1.0 + 3.0 * 0.044715 * pre * pre
            )
            grad = (cot_ref[:, at].astype(f32) * slope).astype(bf16)
            grad_ref[:, base + d * size:base + (d + 1) * size] = grad
            if part:
                pieces[chunk][:, d * size:(d + 1) * size] = grad
            if d % 2:
                to = d // 2 * size
                halves[chunk][:, to:to + size] = jnp.where(xl == 0, grad, even)
            else:
                even = grad


def gelu_pair(xl, own, core, far, cot, part, earlier, wait):
    rows = 64
    steps = H // rows
    whole = lambda w: pl.BlockSpec((rows, w), lambda i, x: (i + part * steps, 0))
    local = lambda w: pl.BlockSpec((rows, w), lambda i, x: (i, 0))
    widths = [width(chunk) for chunk in range(N)]
    extra = widths if part else []
    grid_spec = pltpu.PrefetchScalarGridSpec(
        num_scalar_prefetch=1,
        grid=(steps,),
        in_specs=[local(F)] * 3 + [whole(F)] + [ANY] * (len(earlier) + len(wait)),
        out_specs=[whole(F)] + [whole(w // 2) for w in widths] + [local(w) for w in [F] + extra],
    )
    return pl.pallas_call(
        lambda *refs: gelu_kernel(part, *refs),
        grid_spec=grid_spec,
        out_shape=[jax.ShapeDtypeStruct((S, F), bf16)]
        + [jax.ShapeDtypeStruct((S, w // 2), bf16) for w in widths]
        + [jax.ShapeDtypeStruct((H, w), bf16) for w in [F] + extra],
        input_output_aliases={5 + i: i for i in range(len(earlier))},
        compiler_params=PARAMS,
        cost_estimate=cost(TG),
        name="gelu_pair",
    )(xl, own, core, far, cot, *earlier, *wait)


def weight_kernel(size, apart, ids_ref, tk_ref, tx_ref, *refs):
    first, second, other = refs[:4], refs[4:8], refs[8:12]
    outs, pg = refs[-5 if apart else -2:-1], refs[-1]

    @pl.when(pl.program_id(0) == 0)
    def _():
        xl, r = ids_ref[0], ids_ref[1]
        for k in range(4):
            for z in range(4):
                at = pl.multiple_of((2 * z + xl) * size, size)
                for part, grads in enumerate((first, second)):
                    row = (4 * part + k) * H
                    pg[row:row + H, z * size:(z + 1) * size] = grads[k][:, pl.ds(at, size)]
            slot = pl.multiple_of(4 * S + jnp.bitwise_xor(r, k) * S, S)
            pg[pl.ds(slot, S), :] = other[k][...]

    tokens = jnp.concatenate([tk_ref[...], tx_ref[...]], axis=0)
    total = lax.dot_general(tokens, pg[...], (((0,), (0,)), ((), ())), preferred_element_type=f32).astype(bf16)
    pieces = [total[:, z * size:(z + 1) * size] for z in range(4)]
    if apart:
        z = ids_ref[2]
        low = [jnp.where(z % 2 == 0, pieces[m], pieces[m ^ 1]) for m in range(4)]
        for m, ref in enumerate(outs):
            ref[...] = jnp.where(z // 2 == 0, low[m], low[m ^ 2])
    else:
        for m, piece in enumerate(pieces):
            outs[0][m] = piece


def weight_part(ids, tk, tx, first, second, other, chunk, apart, wait):
    rows = 512
    w = width(chunk)
    size = CHUNKS[chunk][1] * LANE
    at = lambda array: place(chunk) // w if array.shape[1] == F else 0
    if apart:
        out_specs = [pl.BlockSpec((rows, size), lambda i, x: (i, 0))] * 4
        out_shape = [jax.ShapeDtypeStruct((K, size), bf16)] * 4
    else:
        out_specs = pl.BlockSpec((4, rows, size), lambda i, x: (0, i, 0))
        out_shape = jax.ShapeDtypeStruct((4, K, size), bf16)
    grid_spec = pltpu.PrefetchScalarGridSpec(
        num_scalar_prefetch=1,
        grid=(K // rows,),
        in_specs=[pl.BlockSpec((4 * S, rows), lambda i, x: (0, i))] * 2
        + [pl.BlockSpec((H, w), lambda i, x, at=at(array): (0, at)) for array in (*first, *second)]
        + [pl.BlockSpec((S, w // 2), lambda i, x: (0, 0))] * 4
        + [ANY] * len(wait),
        out_specs=out_specs,
        scratch_shapes=[pltpu.VMEM((8 * S, w // 2), bf16)],
    )
    return pl.pallas_call(
        lambda *refs: weight_kernel(size, apart, *refs),
        grid_spec=grid_spec,
        out_shape=out_shape,
        compiler_params=PARAMS,
        cost_estimate=cost(TK),
        name="weight_part",
    )(ids, tk, tx, *first, *second, *other, *wait)


def input_kernel(counts, r_ref, *refs):
    total = sum(counts)
    w_ref, out_ref = refs[total], refs[-1]
    w = jnp.concatenate(
        [
            w_ref[:, (d * UNITS + start) * LANE:(d * UNITS + start + units) * LANE]
            for start, units in (CHUNKS[chunk] for chunk in LAID)
            for d in range(DEPTH)
        ],
        axis=1,
    )
    rows = []
    for count in counts:
        rows.append(jnp.concatenate([ref[...] for ref in refs[:count]], axis=1))
        refs = refs[count:]
    lhs = jnp.concatenate(rows, axis=0)
    total = lax.dot_general(lhs, w, (((1,), (1,)), ((), ())), preferred_element_type=f32).astype(bf16)
    for k in range(4):
        out_ref[jnp.bitwise_xor(r_ref[1], k)] = total[k * H:(k + 1) * H, :]


def input_part(ids, grads, weight, part, earlier, wait):
    tile = 512
    arrays = [array for block in grads for array in block]
    counts = [len(block) for block in grads]
    grid_spec = pltpu.PrefetchScalarGridSpec(
        num_scalar_prefetch=1,
        grid=(K // tile,),
        in_specs=[pl.BlockSpec(array.shape, lambda i, q: (0, 0)) for array in arrays]
        + [pl.BlockSpec((tile, F), lambda i, q: (i, 0))]
        + [ANY] * (len(earlier) + len(wait)),
        out_specs=pl.BlockSpec((4, H, tile), lambda i, q: (0, part, i)),
    )
    return pl.pallas_call(
        lambda *refs: input_kernel(counts, *refs),
        grid_spec=grid_spec,
        out_shape=jax.ShapeDtypeStruct((4, S, K), bf16),
        input_output_aliases={len(arrays) + 2: 0} if earlier else {},
        compiler_params=PARAMS,
        cost_estimate=cost(TK),
        name="input_part",
    )(ids, *arrays, weight, *earlier, *wait)


def join_kernel(first_ref, second_ref, wait_ref, out_ref):
    size = first_ref.shape[1]
    out_ref[:, :size] = first_ref[...]
    out_ref[:, size:] = second_ref[...]


def join(first, second, wait):
    rows = 768
    block = lambda size: pl.BlockSpec((rows, size), lambda i: (i, 0))
    sizes = [first.shape[1], second.shape[1]]
    return pl.pallas_call(
        join_kernel,
        grid=(K // rows,),
        in_specs=[block(size) for size in sizes] + [ANY],
        out_specs=block(sum(sizes)),
        out_shape=jax.ShapeDtypeStruct((K, sum(sizes)), bf16),
        compiler_params=PARAMS,
        cost_estimate=cost(TK),
        name="join",
    )(first, second, wait)


def add_kernel(a_ref, b_ref, wait_ref, out_ref):
    out_ref[...] = (a_ref[...].astype(f32) + b_ref[...].astype(f32)).astype(bf16)


def add(a, b, wait):
    block = pl.BlockSpec((H, F // 2), lambda i: (0, i))
    return pl.pallas_call(
        add_kernel,
        grid=(2,),
        in_specs=[block, block, ANY],
        out_specs=block,
        out_shape=jax.ShapeDtypeStruct(a.shape, bf16),
        compiler_params=PARAMS,
        cost_estimate=cost(1),
        name="add",
    )(a, b, wait)


def fold_kernel(in_ref, out_ref):
    total = in_ref[0].astype(f32)
    for n in range(1, in_ref.shape[0]):
        total += in_ref[n].astype(f32)
    out_ref[...] = total.astype(bf16)


def fold(pieces):
    count, rows, columns = pieces.shape
    tile = rows // 2
    return pl.pallas_call(
        fold_kernel,
        grid=(2,),
        in_specs=[pl.BlockSpec((count, tile, columns), lambda i: (0, i, 0))],
        out_specs=pl.BlockSpec((tile, columns), lambda i: (i, 0)),
        out_shape=jax.ShapeDtypeStruct((rows, columns), bf16),
        compiler_params=PARAMS,
        cost_estimate=cost(TK),
        name="fold",
    )(pieces)


def swap(value, axis, mask):
    n = lax.axis_size(axis)
    return lax.ppermute(value, axis, [(i, i ^ mask) for i in range(n)])


def shards(tokens, weight, cotangent):
    xh, core, y, xl, z = (lax.axis_index(a) for a in ("xh", "core", "y", "xl", "z"))
    r = 2 * xh + core
    q = jnp.bitwise_xor(r, y).astype(jnp.int32).reshape(1)
    ids = jnp.stack([xl, r, z]).astype(jnp.int32)

    partner = swap(tokens, "xl", 1)
    tx = lax.all_gather(partner, "y", axis=0, tiled=True)
    mine = [tokens[:H], tokens[H:]]
    around = [[swap(half, "y", m) for m in (1, 2, 3)] for half in mine]
    around[1] = after(around[1], tokens, TE)

    p0, p1, p2, p3, tk = block_partials(q, [mine[0], *around[0]], weight, 0, (), ())
    total = add(p2, swap(p3, "core", 1), around[1][0])
    (far,) = after([swap(total, "xh", 1)], total)
    terms = [p0, swap(p1, "core", 1), far]
    p0, p1, p2, p3, tk = block_partials(q, [mine[1], *around[1]], weight, 1, (tk,), (total, partner))
    total = add(p2, swap(p3, "core", 1), far)
    *shared, first = gelu_pair(ids, *terms, cotangent, 0, (), ())
    terms = [p0, swap(p1, "core", 1), swap(total, "xh", 1)]
    first_far = swap(first, "xh", 1)
    activation, *halves, second, second_a, second_b = gelu_pair(ids, *terms, cotangent, 1, shared, (tx,))
    far = [swap(value, "xh", 1) for value in (second_a, second_b)]
    near = [swap(half, "xl", 1) for half in halves]
    cross = [lax.ppermute(half, ("xh", "xl"), [(i, 3 - i) for i in range(4)]) for half in halves]

    def pairs(values, wait, micros=300):
        return [(value, swap(value, "core", 1)) for value in after(values, wait, micros)]

    (first, first_core), first_far, (second, second_core) = pairs([first, first_far, second], halves[0])
    first = [first, first_core, *first_far]
    dx = input_part(ids, [[value] for value in first], weight, 0, (), (second_core,))
    far[0], near[0], cross[0] = pairs([far[0], near[0], cross[0]], dx)
    own = [second, second_core]
    dw0 = weight_part(ids, tk, tx, first, [*own, *far[0]], [*near[0], *cross[0]], 0, False, ())
    (far[1],) = pairs([far[1]], dw0)
    blocks = [[value] for value in own] + [[far[chunk][c] for chunk in LAID] for c in range(2)]
    dx = input_part(ids, blocks, weight, 1, (dx,), ())
    near[1], cross[1] = pairs([near[1], cross[1]], dx, T4)
    dw1 = weight_part(ids, tk, tx, first, [*own, *far[1]], [*near[1], *cross[1]], 1, False, ())

    (dx,) = after([lax.all_to_all(dx, "y", 0, 0, tiled=True)], total, T5)
    input_grad = fold(dx)
    dw0, dw1 = (lax.psum_scatter(v, "z", scatter_dimension=0, tiled=True)[0] for v in (dw0, dw1))
    weight_grad = join(dw0, dw1, input_grad)
    return activation, input_grad, weight_grad


def solution(mesh):
    split = Mesh(mesh.devices.reshape(2, 2, 4, 4, 2), ("xh", "core", "y", "z", "xl"))
    hidden = P(("z", "xl", "xh", "core"), "y")
    tokens = P(("z", "xl", "y"), ("xh", "core"))
    return jax.shard_map(
        shards,
        mesh=split,
        in_specs=(tokens, P(("xh", "core"), "y"), hidden),
        out_specs=(hidden, tokens, P(("xh", "core"), ("y", "z", "xl"))),
        check_vma=False,
    )
```

```python
import jax
import jax.numpy as jnp
from jax import lax
from jax.experimental import pallas as pl
from jax.experimental.pallas import tpu as pltpu
from jax.sharding import Mesh
from jax.sharding import PartitionSpec as P

K = 1536
F = 3072
S = 256
H = 128
TILE = 1024
DEPTH = 8
LANE = 128
UNITS = F // (DEPTH * LANE)
CHUNKS = ((0, 1), (1, 2))
N = len(CHUNKS)
LAID = (1, 0)
gelu_coef = 0.7978845608028654
bf16 = jnp.bfloat16
f32 = jnp.float32
MIB = 1 << 20
TF, TG, TK, TE, T3, T4, T5 = 0.01, 30, 0.5, 300, 2, 300, 300
ANY = pl.BlockSpec(memory_space=pl.ANY)
PARAMS = pltpu.CompilerParams(vmem_limit_bytes=63 * MIB)


def cost(micros):
    return pl.CostEstimate(flops=int(micros * 1.15e9), bytes_accessed=int(micros * 3.6e6), transcendentals=0)


def width(chunk):
    return DEPTH * CHUNKS[chunk][1] * LANE


def place(chunk):
    return sum(width(other) for other in LAID[:LAID.index(chunk)])


def after_kernel(*refs):
    pass


def after(values, other, micros=300):
    return pl.pallas_call(
        after_kernel,
        in_specs=[ANY] * (len(values) + 1),
        out_specs=[ANY] * len(values),
        out_shape=[jax.ShapeDtypeStruct(value.shape, value.dtype) for value in values],
        input_output_aliases={n: n for n in range(len(values))},
        cost_estimate=cost(micros),
        name="after",
    )(*values, other)


def partial_kernel(q_ref, b0, b1, b2, b3, w_ref, *refs):
    p0_ref, p1_ref, p2_ref, *p3_refs, tk_ref = refs[-(4 + F // TILE):]

    @pl.when(pl.program_id(0) == 0)
    def _():
        q = q_ref[0]
        for m, block in enumerate((b0, b1, b2, b3)):
            slot = pl.multiple_of(jnp.bitwise_xor(q, m) * H, H)
            tk_ref[pl.ds(slot, H), :] = block[...]

    term = jnp.dot(tk_ref[...], w_ref[...], preferred_element_type=f32).astype(bf16)
    for k, ref in enumerate((p0_ref, p1_ref, p2_ref)):
        ref[...] = term[k * H:(k + 1) * H, :]
    for n, ref in enumerate(p3_refs):

        @pl.when(pl.program_id(0) == n)
        def _():
            ref[...] = term[3 * H:, :]


def block_partials(q, blocks, weight, part, earlier, wait):
    steps = F // TILE
    rows = [pl.BlockSpec((H, K), lambda i, q, at=part if block.shape[0] == S else 0: (at, 0)) for block in blocks]
    grid_spec = pltpu.PrefetchScalarGridSpec(
        num_scalar_prefetch=1,
        grid=(steps,),
        in_specs=rows + [pl.BlockSpec((K, TILE), lambda i, q: (0, i))] + [ANY] * (len(earlier) + len(wait)),
        out_specs=[pl.BlockSpec((H, TILE), lambda i, q: (0, i))] * 3
        + [pl.BlockSpec((H, TILE), lambda i, q: (0, 0))] * steps
        + [pl.BlockSpec((4 * H, K), lambda i, q: (part, 0))],
    )
    return pl.pallas_call(
        partial_kernel,
        grid_spec=grid_spec,
        out_shape=[jax.ShapeDtypeStruct((H, F), bf16)] * 3
        + [jax.ShapeDtypeStruct((H, TILE), bf16)] * steps
        + [jax.ShapeDtypeStruct((4 * S, K), bf16)],
        input_output_aliases={6: 3 + steps} if earlier else {},
        compiler_params=PARAMS,
        cost_estimate=cost(TF),
        name="block_partials",
    )(q, *blocks, weight, *earlier, *wait)


def gelu_kernel(part, xl_ref, own_ref, core_ref, far_ref, cot_ref, *refs):
    act_ref, *outs = refs[-(2 + N + part * N):]
    halves, grad_ref, pieces = outs[:N], outs[N], outs[N + 1:]
    xl = xl_ref[0]
    for chunk, (start, units) in enumerate(CHUNKS):
        size = units * LANE
        base = place(chunk)
        for d in range(DEPTH):
            at = slice(d * UNITS * LANE + start * LANE, d * UNITS * LANE + start * LANE + size)
            pre = own_ref[:, at].astype(f32) + core_ref[:, at].astype(f32) + far_ref[:, at].astype(f32)
            inner = gelu_coef * (pre + 0.044715 * pre * pre * pre)
            tangent = jnp.tanh(inner)
            act_ref[:, at] = (0.5 * pre * (1.0 + tangent)).astype(bf16)
            slope = 0.5 * (1.0 + tangent) + 0.5 * pre * (1.0 - tangent * tangent) * gelu_coef * (
                1.0 + 3.0 * 0.044715 * pre * pre
            )
            grad = (cot_ref[:, at].astype(f32) * slope).astype(bf16)
            grad_ref[:, base + d * size:base + (d + 1) * size] = grad
            if part:
                pieces[chunk][:, d * size:(d + 1) * size] = grad
            if d % 2:
                to = d // 2 * size
                halves[chunk][:, to:to + size] = jnp.where(xl == 0, grad, even)
            else:
                even = grad


def gelu_pair(xl, own, core, far, cot, part, earlier, wait):
    rows = 64
    steps = H // rows
    whole = lambda w: pl.BlockSpec((rows, w), lambda i, x: (i + part * steps, 0))
    local = lambda w: pl.BlockSpec((rows, w), lambda i, x: (i, 0))
    widths = [width(chunk) for chunk in range(N)]
    extra = widths if part else []
    grid_spec = pltpu.PrefetchScalarGridSpec(
        num_scalar_prefetch=1,
        grid=(steps,),
        in_specs=[local(F)] * 3 + [whole(F)] + [ANY] * (len(earlier) + len(wait)),
        out_specs=[whole(F)] + [whole(w // 2) for w in widths] + [local(w) for w in [F] + extra],
    )
    return pl.pallas_call(
        lambda *refs: gelu_kernel(part, *refs),
        grid_spec=grid_spec,
        out_shape=[jax.ShapeDtypeStruct((S, F), bf16)]
        + [jax.ShapeDtypeStruct((S, w // 2), bf16) for w in widths]
        + [jax.ShapeDtypeStruct((H, w), bf16) for w in [F] + extra],
        input_output_aliases={5 + i: i for i in range(len(earlier))},
        compiler_params=PARAMS,
        cost_estimate=cost(TG),
        name="gelu_pair",
    )(xl, own, core, far, cot, *earlier, *wait)


def weight_kernel(size, masks, ids_ref, tk_ref, tx_ref, *refs):
    first, second, other = refs[:4], refs[4:8], refs[8:12]
    outs, pg = refs[-(1 + count_outs(masks)):-1], refs[-1]
    shares = masks or range(4)

    @pl.when(pl.program_id(0) == 0)
    def _():
        xl, r, z = ids_ref[0], ids_ref[1], ids_ref[2]
        for n, share in enumerate(shares):
            to = jnp.bitwise_xor(z, share) if masks else share
            cols = slice(n * size, (n + 1) * size)
            own = pl.ds(pl.multiple_of((2 * to + xl) * size, size), size)
            near = pl.ds(pl.multiple_of(to * size, size), size)
            for k in range(4):
                for part, grads in enumerate((first, second)):
                    row = (4 * part + k) * H
                    pg[row:row + H, cols] = grads[k][:, own]
                slot = pl.multiple_of(4 * S + jnp.bitwise_xor(r, k) * S, S)
                pg[pl.ds(slot, S), cols] = other[k][:, near]

    tokens = jnp.concatenate([tk_ref[...], tx_ref[...]], axis=0)
    total = lax.dot_general(tokens, pg[...], (((0,), (0,)), ((), ())), preferred_element_type=f32).astype(bf16)
    if len(shares) == 1:
        for n, out_ref in enumerate(outs):

            @pl.when(pl.program_id(0) == n)
            def _():
                out_ref[...] = total

    else:
        for n in range(len(shares)):
            piece = total[:, n * size:(n + 1) * size]
            if masks:
                outs[n][...] = piece
            else:
                outs[0][n] = piece


def count_outs(masks):
    return max(2, len(masks)) if masks else 1


def weight_part(ids, tk, tx, first, second, other, chunk, masks, wait):
    w = width(chunk)
    size = CHUNKS[chunk][1] * LANE
    rows = K // 2 if len(masks) == 1 else 512
    at = lambda array: place(chunk) // w if array.shape[1] == F else 0
    if len(masks) == 1:
        out_specs = [pl.BlockSpec((rows, size), lambda i, x: (0, 0))] * 2
        out_shape = [jax.ShapeDtypeStruct((rows, size), bf16)] * 2
    elif masks:
        out_specs = [pl.BlockSpec((rows, size), lambda i, x: (i, 0))] * len(masks)
        out_shape = [jax.ShapeDtypeStruct((K, size), bf16)] * len(masks)
    else:
        out_specs = pl.BlockSpec((4, rows, size), lambda i, x: (0, i, 0))
        out_shape = jax.ShapeDtypeStruct((4, K, size), bf16)
    grid_spec = pltpu.PrefetchScalarGridSpec(
        num_scalar_prefetch=1,
        grid=(K // rows,),
        in_specs=[pl.BlockSpec((4 * S, rows), lambda i, x: (0, i))] * 2
        + [pl.BlockSpec((H, w), lambda i, x, at=at(array): (0, at)) for array in (*first, *second)]
        + [pl.BlockSpec((S, w // 2), lambda i, x: (0, 0))] * 4
        + [ANY] * len(wait),
        out_specs=out_specs,
        scratch_shapes=[pltpu.VMEM((8 * S, size * (len(masks) or 4)), bf16)],
    )
    return pl.pallas_call(
        lambda *refs: weight_kernel(size, masks, *refs),
        grid_spec=grid_spec,
        out_shape=out_shape,
        compiler_params=PARAMS,
        cost_estimate=cost(TK),
        name="weight_part",
    )(ids, tk, tx, *first, *second, *other, *wait)


def relay_kernel(a_ref, b_ref, last_ref, first_ref, a_out, b_out):
    a_out[...] = (a_ref[...].astype(f32) + last_ref[...].astype(f32)).astype(bf16)
    b_out[...] = (b_ref[...].astype(f32) + first_ref[...].astype(f32)).astype(bf16)


def relay(a, b, last, first):
    rows, columns = last.shape[0] // 2, last.shape[1]
    top = pl.BlockSpec((rows, columns), lambda i: (i, 0))
    bottom = pl.BlockSpec((rows, columns), lambda i: (i + 2, 0))
    return pl.pallas_call(
        relay_kernel,
        grid=(2,),
        in_specs=[bottom, top, top, top],
        out_specs=[bottom, top],
        out_shape=[jax.ShapeDtypeStruct(a.shape, bf16)] * 2,
        input_output_aliases={0: 0, 1: 1},
        compiler_params=PARAMS,
        cost_estimate=cost(TK),
        name="relay",
    )(a, b, last, first)


def input_kernel(counts, r_ref, *refs):
    total = sum(counts)
    w_ref, out_ref = refs[total], refs[-1]
    w = jnp.concatenate(
        [
            w_ref[:, (d * UNITS + start) * LANE:(d * UNITS + start + units) * LANE]
            for start, units in (CHUNKS[chunk] for chunk in LAID)
            for d in range(DEPTH)
        ],
        axis=1,
    )
    rows = []
    for count in counts:
        rows.append(jnp.concatenate([ref[...] for ref in refs[:count]], axis=1))
        refs = refs[count:]
    lhs = jnp.concatenate(rows, axis=0)
    total = lax.dot_general(lhs, w, (((1,), (1,)), ((), ())), preferred_element_type=f32).astype(bf16)
    for k in range(4):
        out_ref[jnp.bitwise_xor(r_ref[1], k)] = total[k * H:(k + 1) * H, :]


def input_part(ids, grads, weight, part, earlier, wait):
    tile = 512
    arrays = [array for block in grads for array in block]
    counts = [len(block) for block in grads]
    grid_spec = pltpu.PrefetchScalarGridSpec(
        num_scalar_prefetch=1,
        grid=(K // tile,),
        in_specs=[pl.BlockSpec(array.shape, lambda i, q: (0, 0)) for array in arrays]
        + [pl.BlockSpec((tile, F), lambda i, q: (i, 0))]
        + [ANY] * (len(earlier) + len(wait)),
        out_specs=pl.BlockSpec((4, H, tile), lambda i, q: (0, part, i)),
    )
    return pl.pallas_call(
        lambda *refs: input_kernel(counts, *refs),
        grid_spec=grid_spec,
        out_shape=jax.ShapeDtypeStruct((4, S, K), bf16),
        input_output_aliases={len(arrays) + 2: 0} if earlier else {},
        compiler_params=PARAMS,
        cost_estimate=cost(TK),
        name="input_part",
    )(ids, *arrays, weight, *earlier, *wait)


def join_kernel(first_ref, *refs):
    size = first_ref.shape[1]
    total = refs[0][...].astype(f32)
    for ref in refs[1:-1]:
        total += ref[...].astype(f32)
    refs[-1][:, :size] = first_ref[...]
    refs[-1][:, size:] = total.astype(bf16)


def join(first, pieces, wait):
    rows = 512
    block = lambda size: pl.BlockSpec((rows, size), lambda i: (i, 0))
    sizes = [first.shape[1], pieces[0].shape[1]]
    return pl.pallas_call(
        lambda *refs: join_kernel(*refs[:1 + len(pieces)], refs[-1]),
        grid=(K // rows,),
        in_specs=[block(sizes[0])] + [block(sizes[1])] * len(pieces) + [ANY],
        out_specs=block(sum(sizes)),
        out_shape=jax.ShapeDtypeStruct((K, sum(sizes)), bf16),
        compiler_params=PARAMS,
        cost_estimate=cost(TK),
        name="join",
    )(first, *pieces, wait)


def add_kernel(a_ref, *refs):
    out_ref = refs[-1]
    for n in range(F // TILE):

        @pl.when(pl.program_id(0) == n)
        def _():
            out_ref[...] = (a_ref[...].astype(f32) + refs[n][...].astype(f32)).astype(bf16)


def add(a, pieces, wait):
    block = pl.BlockSpec((H, TILE), lambda i: (0, i))
    return pl.pallas_call(
        add_kernel,
        grid=(F // TILE,),
        in_specs=[block] + [pl.BlockSpec((H, TILE), lambda i: (0, 0))] * len(pieces) + [ANY],
        out_specs=block,
        out_shape=jax.ShapeDtypeStruct(a.shape, bf16),
        compiler_params=PARAMS,
        cost_estimate=cost(1),
        name="add",
    )(a, *pieces, wait)


def fold_kernel(in_ref, out_ref):
    total = in_ref[0].astype(f32)
    for n in range(1, in_ref.shape[0]):
        total += in_ref[n].astype(f32)
    out_ref[...] = total.astype(bf16)


def fold(pieces):
    count, rows, columns = pieces.shape
    tile = rows // 2
    return pl.pallas_call(
        fold_kernel,
        grid=(2,),
        in_specs=[pl.BlockSpec((count, tile, columns), lambda i: (0, i, 0))],
        out_specs=pl.BlockSpec((tile, columns), lambda i: (i, 0)),
        out_shape=jax.ShapeDtypeStruct((rows, columns), bf16),
        compiler_params=PARAMS,
        cost_estimate=cost(TK),
        name="fold",
    )(pieces)


def swap(value, axis, mask):
    n = lax.axis_size(axis)
    return lax.ppermute(value, axis, [(i, i ^ mask) for i in range(n)])


def shards(tokens, weight, cotangent):
    xh, core, y, xl, z = (lax.axis_index(a) for a in ("xh", "core", "y", "xl", "z"))
    r = 2 * xh + core
    q = jnp.bitwise_xor(r, y).astype(jnp.int32).reshape(1)
    ids = jnp.stack([xl, r, z]).astype(jnp.int32)

    partner = swap(tokens, "xl", 1)
    tx = lax.all_gather(partner, "y", axis=0, tiled=True)
    mine = [tokens[:H], tokens[H:]]
    around = [[swap(half, "y", m) for m in (1, 2, 3)] for half in mine]
    around[1] = after(around[1], tokens, TE)

    p0, p1, p2, *p3, tk = block_partials(q, [mine[0], *around[0]], weight, 0, (), ())
    total = add(p2, [swap(v, "core", 1) for v in p3], around[1][0])
    (far,) = after([swap(total, "xh", 1)], total, T3)
    terms = [p0, swap(p1, "core", 1), far]
    p0, p1, p2, *p3, tk = block_partials(q, [mine[1], *around[1]], weight, 1, (tk,), (total, partner))
    total = add(p2, [swap(v, "core", 1) for v in p3], total)
    *shared, first = gelu_pair(ids, *terms, cotangent, 0, (), ())
    terms = [p0, swap(p1, "core", 1), swap(total, "xh", 1)]
    first_far = swap(first, "xh", 1)
    activation, *halves, second, second_a, second_b = gelu_pair(ids, *terms, cotangent, 1, shared, ())
    far = [swap(value, "xh", 1) for value in (second_a, second_b)]
    near = [swap(half, "xl", 1) for half in halves]
    cross = [lax.ppermute(half, ("xh", "xl"), [(i, 3 - i) for i in range(4)]) for half in halves]

    def pairs(values, wait, micros=300):
        return [(value, swap(value, "core", 1)) for value in after(values, wait, micros)]

    (first, first_core), first_far, (second, second_core) = pairs([first, first_far, second], halves[0])
    first = [first, first_core, *first_far]
    dx = input_part(ids, [[value] for value in first], weight, 0, (), (second_core, tx))
    far[0], near[0], cross[0] = pairs([far[0], near[0], cross[0]], dx)
    own = [second, second_core]
    dw0 = weight_part(ids, tk, tx, first, [*own, *far[0]], [*near[0], *cross[0]], 0, (), ())
    (far[1],) = pairs([far[1]], dw0)
    blocks = [[value] for value in own] + [[far[chunk][c] for chunk in LAID] for c in range(2)]
    dx = input_part(ids, blocks, weight, 1, (dx,), ())
    near[1], cross[1] = pairs([near[1], cross[1]], dx, T4)
    dw0 = lax.psum_scatter(dw0, "z", scatter_dimension=0, tiled=True)[0]
    last = [first, [*own, *far[1]], [*near[1], *cross[1]], 1]
    top, bottom = weight_part(ids, tk, tx, *last, (2,), ())
    to_right, to_left = swap(top, "z", 1), swap(bottom, "z", 3)
    mine, one, three = weight_part(ids, tk, tx, *last, (0, 1, 3), (top, dw0))
    one, three = relay(one, three, to_left, to_right)

    (dx,) = after([lax.all_to_all(dx, "y", 0, 0, tiled=True)], total, T5)
    input_grad = fold(dx)
    weight_grad = join(dw0, [mine, swap(one, "z", 1), swap(three, "z", 3)], input_grad)
    return activation, input_grad, weight_grad


def solution(mesh):
    split = Mesh(mesh.devices.reshape(2, 2, 4, 4, 2), ("xh", "core", "y", "z", "xl"))
    hidden = P(("z", "xl", "xh", "core"), "y")
    tokens = P(("z", "xl", "y"), ("xh", "core"))
    return jax.shard_map(
        shards,
        mesh=split,
        in_specs=(tokens, P(("xh", "core"), "y"), hidden),
        out_specs=(hidden, tokens, P(("xh", "core"), ("y", "z", "xl"))),
        check_vma=False,
    )
```

```python
import jax
import jax.numpy as jnp
from jax import lax
from jax.experimental import pallas as pl
from jax.experimental.pallas import tpu as pltpu
from jax.sharding import Mesh
from jax.sharding import PartitionSpec as P

K = 1536
F = 3072
S = 256
H = 128
TILE = 1024
DEPTH = 8
LANE = 128
UNITS = F // (DEPTH * LANE)
CHUNKS = ((0, 1), (1, 2))
N = len(CHUNKS)
LAID = (1, 0)
gelu_coef = 0.7978845608028654
bf16 = jnp.bfloat16
f32 = jnp.float32
MIB = 1 << 20
TF, TG, TK, TE, T3, T4, T5 = 0.01, 30, 0.5, 300, 2, 300, 300
ANY = pl.BlockSpec(memory_space=pl.ANY)
PARAMS = pltpu.CompilerParams(vmem_limit_bytes=63 * MIB)


def cost(micros):
    return pl.CostEstimate(flops=int(micros * 1.15e9), bytes_accessed=int(micros * 3.6e6), transcendentals=0)


def width(chunk):
    return DEPTH * CHUNKS[chunk][1] * LANE


def place(chunk):
    return sum(width(other) for other in LAID[:LAID.index(chunk)])


def after_kernel(*refs):
    pass


def after(values, other, micros=300):
    return pl.pallas_call(
        after_kernel,
        in_specs=[ANY] * (len(values) + 1),
        out_specs=[ANY] * len(values),
        out_shape=[jax.ShapeDtypeStruct(value.shape, value.dtype) for value in values],
        input_output_aliases={n: n for n in range(len(values))},
        cost_estimate=cost(micros),
        name="after",
    )(*values, other)


def partial_kernel(q_ref, b0, b1, b2, b3, w_ref, *refs):
    p0_ref, p1_ref, p2_ref, *p3_refs, tk_ref = refs[-(4 + F // TILE):]

    @pl.when(pl.program_id(0) == 0)
    def _():
        q = q_ref[0]
        for m, block in enumerate((b0, b1, b2, b3)):
            slot = pl.multiple_of(jnp.bitwise_xor(q, m) * H, H)
            tk_ref[pl.ds(slot, H), :] = block[...]

    term = jnp.dot(tk_ref[...], w_ref[...], preferred_element_type=f32).astype(bf16)
    for k, ref in enumerate((p0_ref, p1_ref, p2_ref)):
        ref[...] = term[k * H:(k + 1) * H, :]
    for n, ref in enumerate(p3_refs):

        @pl.when(pl.program_id(0) == n)
        def _():
            ref[...] = term[3 * H:, :]


def block_partials(q, blocks, weight, part, earlier, wait):
    steps = F // TILE
    rows = [pl.BlockSpec((H, K), lambda i, q, at=part if block.shape[0] == S else 0: (at, 0)) for block in blocks]
    grid_spec = pltpu.PrefetchScalarGridSpec(
        num_scalar_prefetch=1,
        grid=(steps,),
        in_specs=rows + [pl.BlockSpec((K, TILE), lambda i, q: (0, i))] + [ANY] * (len(earlier) + len(wait)),
        out_specs=[pl.BlockSpec((H, TILE), lambda i, q: (0, i))] * 3
        + [pl.BlockSpec((H, TILE), lambda i, q: (0, 0))] * steps
        + [pl.BlockSpec((4 * H, K), lambda i, q: (part, 0))],
    )
    return pl.pallas_call(
        partial_kernel,
        grid_spec=grid_spec,
        out_shape=[jax.ShapeDtypeStruct((H, F), bf16)] * 3
        + [jax.ShapeDtypeStruct((H, TILE), bf16)] * steps
        + [jax.ShapeDtypeStruct((4 * S, K), bf16)],
        input_output_aliases={6: 3 + steps} if earlier else {},
        compiler_params=PARAMS,
        cost_estimate=cost(TF),
        name="block_partials",
    )(q, *blocks, weight, *earlier, *wait)


def gelu_kernel(part, xl_ref, own_ref, core_ref, far_ref, cot_ref, *refs):
    act_ref, *outs = refs[-(2 + N + part * N):]
    halves, grad_ref, pieces = outs[:N], outs[N], outs[N + 1:]
    xl = xl_ref[0]
    for chunk, (start, units) in enumerate(CHUNKS):
        size = units * LANE
        base = place(chunk)
        for d in range(DEPTH):
            at = slice(d * UNITS * LANE + start * LANE, d * UNITS * LANE + start * LANE + size)
            pre = own_ref[:, at].astype(f32) + core_ref[:, at].astype(f32) + far_ref[:, at].astype(f32)
            inner = gelu_coef * (pre + 0.044715 * pre * pre * pre)
            tangent = jnp.tanh(inner)
            act_ref[:, at] = (0.5 * pre * (1.0 + tangent)).astype(bf16)
            slope = 0.5 * (1.0 + tangent) + 0.5 * pre * (1.0 - tangent * tangent) * gelu_coef * (
                1.0 + 3.0 * 0.044715 * pre * pre
            )
            grad = (cot_ref[:, at].astype(f32) * slope).astype(bf16)
            grad_ref[:, base + d * size:base + (d + 1) * size] = grad
            if part:
                pieces[chunk][:, d * size:(d + 1) * size] = grad
            if d % 2:
                to = d // 2 * size
                halves[chunk][:, to:to + size] = jnp.where(xl == 0, grad, even)
            else:
                even = grad


def gelu_pair(xl, own, core, far, cot, part, earlier, wait):
    rows = 64
    steps = H // rows
    whole = lambda w: pl.BlockSpec((rows, w), lambda i, x: (i + part * steps, 0))
    local = lambda w: pl.BlockSpec((rows, w), lambda i, x: (i, 0))
    widths = [width(chunk) for chunk in range(N)]
    extra = widths if part else []
    grid_spec = pltpu.PrefetchScalarGridSpec(
        num_scalar_prefetch=1,
        grid=(steps,),
        in_specs=[local(F)] * 3 + [whole(F)] + [ANY] * (len(earlier) + len(wait)),
        out_specs=[whole(F)] + [whole(w // 2) for w in widths] + [local(w) for w in [F] + extra],
    )
    return pl.pallas_call(
        lambda *refs: gelu_kernel(part, *refs),
        grid_spec=grid_spec,
        out_shape=[jax.ShapeDtypeStruct((S, F), bf16)]
        + [jax.ShapeDtypeStruct((S, w // 2), bf16) for w in widths]
        + [jax.ShapeDtypeStruct((H, w), bf16) for w in [F] + extra],
        input_output_aliases={5 + i: i for i in range(len(earlier))},
        compiler_params=PARAMS,
        cost_estimate=cost(TG),
        name="gelu_pair",
    )(xl, own, core, far, cot, *earlier, *wait)


def weight_kernel(size, masks, halves, ids_ref, tk_ref, tx_ref, *refs):
    count = max(1, len(masks))
    groups = [refs[12 * n:12 * (n + 1)] for n in range(count)]
    outs, pg = refs[-(1 + count * (1 + halves)):-1], refs[-1]

    @pl.when(pl.program_id(0) == 0)
    def _():
        xl, r = ids_ref[0], ids_ref[1]
        for n in range(len(masks) or 4):
            cols = slice(n * size, (n + 1) * size)
            own = near = slice(None)
            if not masks:
                own = pl.ds(pl.multiple_of((2 * n + xl) * size, size), size)
                near = cols
            group = groups[n if masks else 0]
            for k in range(4):
                for part in range(2):
                    row = (4 * part + k) * H
                    pg[row:row + H, cols] = group[4 * part + k][:, own]
                slot = pl.multiple_of(4 * S + jnp.bitwise_xor(r, k) * S, S)
                pg[pl.ds(slot, S), cols] = group[8 + k][:, near]

    tokens = jnp.concatenate([tk_ref[...], tx_ref[...]], axis=0)
    total = lax.dot_general(tokens, pg[...], (((0,), (0,)), ((), ())), preferred_element_type=f32).astype(bf16)
    if halves:
        for n, out_ref in enumerate(outs):

            @pl.when(pl.program_id(0) == n)
            def _():
                out_ref[...] = total

    else:
        for n in range(len(masks) or 4):
            piece = total[:, n * size:(n + 1) * size]
            if masks:
                outs[n][...] = piece
            else:
                outs[0][n] = piece


def weight_part(ids, tk, tx, first, second, other, chunk, masks, halves, wait):
    w = width(chunk)
    size = CHUNKS[chunk][1] * LANE
    rows = K // 2 if len(masks) == 1 else 512
    specs = []
    for m in masks:
        for array in (*first, *second):
            at = place(chunk) // size if array.shape[1] == F else 0
            specs.append(
                pl.BlockSpec((H, size), lambda i, x, at=at, m=m: (0, at + 2 * jnp.bitwise_xor(x[2], m) + x[0]))
            )
        specs += [pl.BlockSpec((S, size), lambda i, x, m=m: (0, jnp.bitwise_xor(x[2], m)))] * 4
    if not masks:
        for array in (*first, *second):
            at = place(chunk) // w if array.shape[1] == F else 0
            specs.append(pl.BlockSpec((H, w), lambda i, x, at=at: (0, at)))
        specs += [pl.BlockSpec((S, w // 2), lambda i, x: (0, 0))] * 4
    if halves:
        out_specs = [pl.BlockSpec((rows, size), lambda i, x: (0, 0))] * 2
        out_shape = [jax.ShapeDtypeStruct((rows, size), bf16)] * 2
    elif masks:
        out_specs = [pl.BlockSpec((rows, size), lambda i, x: (i, 0))] * len(masks)
        out_shape = [jax.ShapeDtypeStruct((K, size), bf16)] * len(masks)
    else:
        out_specs = pl.BlockSpec((4, rows, size), lambda i, x: (0, i, 0))
        out_shape = jax.ShapeDtypeStruct((4, K, size), bf16)
    grid_spec = pltpu.PrefetchScalarGridSpec(
        num_scalar_prefetch=1,
        grid=(K // rows,),
        in_specs=[pl.BlockSpec((4 * S, rows), lambda i, x: (0, i))] * 2 + specs + [ANY] * len(wait),
        out_specs=out_specs,
        scratch_shapes=[pltpu.VMEM((8 * S, size * (len(masks) or 4)), bf16)],
    )
    return pl.pallas_call(
        lambda *refs: weight_kernel(size, masks, halves, *refs),
        grid_spec=grid_spec,
        out_shape=out_shape,
        compiler_params=PARAMS,
        cost_estimate=cost(TK),
        name="weight_part",
    )(ids, tk, tx, *([*first, *second, *other] * max(1, len(masks))), *wait)


def relay_kernel(a_ref, b_ref, last_ref, first_ref, a_out, b_out):
    a_out[...] = (a_ref[...].astype(f32) + last_ref[...].astype(f32)).astype(bf16)
    b_out[...] = (b_ref[...].astype(f32) + first_ref[...].astype(f32)).astype(bf16)


def relay(a, b, last, first):
    rows, columns = last.shape[0] // 2, last.shape[1]
    top = pl.BlockSpec((rows, columns), lambda i: (i, 0))
    bottom = pl.BlockSpec((rows, columns), lambda i: (i + 2, 0))
    return pl.pallas_call(
        relay_kernel,
        grid=(2,),
        in_specs=[bottom, top, top, top],
        out_specs=[bottom, top],
        out_shape=[jax.ShapeDtypeStruct(a.shape, bf16)] * 2,
        input_output_aliases={0: 0, 1: 1},
        compiler_params=PARAMS,
        cost_estimate=cost(TK),
        name="relay",
    )(a, b, last, first)


def input_kernel(counts, r_ref, *refs):
    total = sum(counts)
    w_ref, out_ref = refs[total], refs[-1]
    w = jnp.concatenate(
        [
            w_ref[:, (d * UNITS + start) * LANE:(d * UNITS + start + units) * LANE]
            for start, units in (CHUNKS[chunk] for chunk in LAID)
            for d in range(DEPTH)
        ],
        axis=1,
    )
    rows = []
    for count in counts:
        rows.append(jnp.concatenate([ref[...] for ref in refs[:count]], axis=1))
        refs = refs[count:]
    lhs = jnp.concatenate(rows, axis=0)
    total = lax.dot_general(lhs, w, (((1,), (1,)), ((), ())), preferred_element_type=f32).astype(bf16)
    for k in range(4):
        out_ref[jnp.bitwise_xor(r_ref[1], k)] = total[k * H:(k + 1) * H, :]


def input_part(ids, grads, weight, part, earlier, wait):
    tile = 512
    arrays = [array for block in grads for array in block]
    counts = [len(block) for block in grads]
    grid_spec = pltpu.PrefetchScalarGridSpec(
        num_scalar_prefetch=1,
        grid=(K // tile,),
        in_specs=[pl.BlockSpec(array.shape, lambda i, q: (0, 0)) for array in arrays]
        + [pl.BlockSpec((tile, F), lambda i, q: (i, 0))]
        + [ANY] * (len(earlier) + len(wait)),
        out_specs=pl.BlockSpec((4, H, tile), lambda i, q: (0, part, i)),
    )
    return pl.pallas_call(
        lambda *refs: input_kernel(counts, *refs),
        grid_spec=grid_spec,
        out_shape=jax.ShapeDtypeStruct((4, S, K), bf16),
        input_output_aliases={len(arrays) + 2: 0} if earlier else {},
        compiler_params=PARAMS,
        cost_estimate=cost(TK),
        name="input_part",
    )(ids, *arrays, weight, *earlier, *wait)


def join_kernel(first_ref, *refs):
    size = first_ref.shape[1]
    total = refs[0][...].astype(f32)
    for ref in refs[1:-1]:
        total += ref[...].astype(f32)
    refs[-1][:, :size] = first_ref[...]
    refs[-1][:, size:] = total.astype(bf16)


def join(first, pieces, wait):
    rows = 768
    block = lambda size: pl.BlockSpec((rows, size), lambda i: (i, 0))
    sizes = [first.shape[1], pieces[0].shape[1]]
    return pl.pallas_call(
        lambda *refs: join_kernel(*refs[:1 + len(pieces)], refs[-1]),
        grid=(K // rows,),
        in_specs=[block(sizes[0])] + [block(sizes[1])] * len(pieces) + [ANY],
        out_specs=block(sum(sizes)),
        out_shape=jax.ShapeDtypeStruct((K, sum(sizes)), bf16),
        compiler_params=PARAMS,
        cost_estimate=cost(TK),
        name="join",
    )(first, *pieces, wait)


def add_kernel(a_ref, *refs):
    out_ref = refs[-1]
    for n in range(F // TILE):
        at = slice(n * TILE, (n + 1) * TILE)
        out_ref[:, at] = (a_ref[:, at].astype(f32) + refs[n][...].astype(f32)).astype(bf16)


def add(a, pieces, wait):
    block = pl.BlockSpec((H, F), lambda i: (0, 0))
    return pl.pallas_call(
        add_kernel,
        grid=(1,),
        in_specs=[block] + [pl.BlockSpec((H, TILE), lambda i: (0, 0))] * len(pieces) + [ANY],
        out_specs=block,
        out_shape=jax.ShapeDtypeStruct(a.shape, bf16),
        compiler_params=PARAMS,
        cost_estimate=cost(1),
        name="add",
    )(a, *pieces, wait)


def fold_kernel(in_ref, out_ref):
    total = in_ref[0].astype(f32)
    for n in range(1, in_ref.shape[0]):
        total += in_ref[n].astype(f32)
    out_ref[...] = total.astype(bf16)


def fold(pieces):
    count, rows, columns = pieces.shape
    tile = rows // 2
    return pl.pallas_call(
        fold_kernel,
        grid=(2,),
        in_specs=[pl.BlockSpec((count, tile, columns), lambda i: (0, i, 0))],
        out_specs=pl.BlockSpec((tile, columns), lambda i: (i, 0)),
        out_shape=jax.ShapeDtypeStruct((rows, columns), bf16),
        compiler_params=PARAMS,
        cost_estimate=cost(TK),
        name="fold",
    )(pieces)


def swap(value, axis, mask):
    n = lax.axis_size(axis)
    return lax.ppermute(value, axis, [(i, i ^ mask) for i in range(n)])


def shards(tokens, weight, cotangent):
    xh, core, y, xl, z = (lax.axis_index(a) for a in ("xh", "core", "y", "xl", "z"))
    r = 2 * xh + core
    q = jnp.bitwise_xor(r, y).astype(jnp.int32).reshape(1)
    ids = jnp.stack([xl, r, z]).astype(jnp.int32)

    partner = swap(tokens, "xl", 1)
    tx = lax.all_gather(partner, "y", axis=0, tiled=True)
    mine = [tokens[:H], tokens[H:]]
    around = [[swap(half, "y", m) for m in (1, 2, 3)] for half in mine]
    around[1] = after(around[1], tokens, TE)

    p0, p1, p2, *p3, tk = block_partials(q, [mine[0], *around[0]], weight, 0, (), ())
    total = add(p2, [swap(v, "core", 1) for v in p3], around[1][0])
    (far,) = after([swap(total, "xh", 1)], total, T3)
    terms = [p0, swap(p1, "core", 1), far]
    p0, p1, p2, *p3, tk = block_partials(q, [mine[1], *around[1]], weight, 1, (tk,), (total, partner))
    total = add(p2, [swap(v, "core", 1) for v in p3], total)
    *shared, first = gelu_pair(ids, *terms, cotangent, 0, (), ())
    terms = [p0, swap(p1, "core", 1), swap(total, "xh", 1)]
    first_far = swap(first, "xh", 1)
    activation, *halves, second, second_a, second_b = gelu_pair(ids, *terms, cotangent, 1, shared, ())
    far = [swap(value, "xh", 1) for value in (second_a, second_b)]
    near = [swap(half, "xl", 1) for half in halves]
    cross = [lax.ppermute(half, ("xh", "xl"), [(i, 3 - i) for i in range(4)]) for half in halves]

    def pairs(values, wait, micros=300):
        return [(value, swap(value, "core", 1)) for value in after(values, wait, micros)]

    (first, first_core), first_far, (second, second_core) = pairs([first, first_far, second], halves[0])
    first = [first, first_core, *first_far]
    dx = input_part(ids, [[value] for value in first], weight, 0, (), (second_core, tx))
    far[0], near[0], cross[0] = pairs([far[0], near[0], cross[0]], dx)
    own = [second, second_core]
    dw0 = weight_part(ids, tk, tx, first, [*own, *far[0]], [*near[0], *cross[0]], 0, (), False, ())
    (far[1],) = pairs([far[1]], dw0)
    blocks = [[value] for value in own] + [[far[chunk][c] for chunk in LAID] for c in range(2)]
    dx = input_part(ids, blocks, weight, 1, (dx,), ())
    near[1], cross[1] = pairs([near[1], cross[1]], dx, T4)
    dw0 = lax.psum_scatter(dw0, "z", scatter_dimension=0, tiled=True)[0]
    last = [first, [*own, *far[1]], [*near[1], *cross[1]], 1]
    top, bottom = weight_part(ids, tk, tx, *last, (2,), True, ())
    to_right, to_left = swap(top, "z", 1), swap(bottom, "z", 3)
    one, three = weight_part(ids, tk, tx, *last, (1, 3), False, (top, dw0))
    one, three = relay(one, three, to_left, to_right)
    (mine,) = weight_part(ids, tk, tx, *last, (0,), False, (one,))

    (dx,) = after([lax.all_to_all(dx, "y", 0, 0, tiled=True)], total, T5)
    input_grad = fold(dx)
    weight_grad = join(dw0, [mine, swap(one, "z", 1), swap(three, "z", 3)], input_grad)
    return activation, input_grad, weight_grad


def solution(mesh):
    split = Mesh(mesh.devices.reshape(2, 2, 4, 4, 2), ("xh", "core", "y", "z", "xl"))
    hidden = P(("z", "xl", "xh", "core"), "y")
    tokens = P(("z", "xl", "y"), ("xh", "core"))
    return jax.shard_map(
        shards,
        mesh=split,
        in_specs=(tokens, P(("xh", "core"), "y"), hidden),
        out_specs=(hidden, tokens, P(("xh", "core"), ("y", "z", "xl"))),
        check_vma=False,
    )
```

```python
import jax
import jax.numpy as jnp
from jax import lax
from jax.experimental import pallas as pl
from jax.experimental.pallas import tpu as pltpu
from jax.sharding import Mesh
from jax.sharding import PartitionSpec as P

K = 1536
F = 3072
S = 256
H = 128
TILE = 1024
DEPTH = 8
LANE = 128
UNITS = F // (DEPTH * LANE)
CHUNKS = ((0, 1), (1, 2))
N = len(CHUNKS)
LAID = (1, 0)
gelu_coef = 0.7978845608028654
bf16 = jnp.bfloat16
f32 = jnp.float32
MIB = 1 << 20
TF, TG, TK, TE, T3, T4, T5 = 0.01, 30, 0.5, 300, 2, 300, 300
ANY = pl.BlockSpec(memory_space=pl.ANY)
PARAMS = pltpu.CompilerParams(vmem_limit_bytes=64 * MIB)


def cost(micros):
    return pl.CostEstimate(flops=int(micros * 1.15e9), bytes_accessed=int(micros * 3.6e6), transcendentals=0)


def width(chunk):
    return DEPTH * CHUNKS[chunk][1] * LANE


def place(chunk):
    return sum(width(other) for other in LAID[:LAID.index(chunk)])


def after_kernel(*refs):
    pass


def after(values, other, micros=300):
    return pl.pallas_call(
        after_kernel,
        in_specs=[ANY] * (len(values) + 1),
        out_specs=[ANY] * len(values),
        out_shape=[jax.ShapeDtypeStruct(value.shape, value.dtype) for value in values],
        input_output_aliases={n: n for n in range(len(values))},
        cost_estimate=cost(micros),
        name="after",
    )(*values, other)


def partial_kernel(q_ref, b0, b1, b2, b3, w_ref, *refs):
    p0_ref, p1_ref, p2_ref, *p3_refs, tk_ref = refs[-(4 + F // TILE):]

    @pl.when(pl.program_id(0) == 0)
    def _():
        q = q_ref[0]
        for m, block in enumerate((b0, b1, b2, b3)):
            slot = pl.multiple_of(jnp.bitwise_xor(q, m) * H, H)
            tk_ref[pl.ds(slot, H), :] = block[...]

    term = jnp.dot(tk_ref[...], w_ref[...], preferred_element_type=f32).astype(bf16)
    for k, ref in enumerate((p0_ref, p1_ref, p2_ref)):
        ref[...] = term[k * H:(k + 1) * H, :]
    for n, ref in enumerate(p3_refs):

        @pl.when(pl.program_id(0) == n)
        def _():
            ref[...] = term[3 * H:, :]


def block_partials(q, blocks, weight, part, earlier, wait):
    steps = F // TILE
    rows = [pl.BlockSpec((H, K), lambda i, q, at=part if block.shape[0] == S else 0: (at, 0)) for block in blocks]
    grid_spec = pltpu.PrefetchScalarGridSpec(
        num_scalar_prefetch=1,
        grid=(steps,),
        in_specs=rows + [pl.BlockSpec((K, TILE), lambda i, q: (0, i))] + [ANY] * (len(earlier) + len(wait)),
        out_specs=[pl.BlockSpec((H, TILE), lambda i, q: (0, i))] * 3
        + [pl.BlockSpec((H, TILE), lambda i, q: (0, 0))] * steps
        + [pl.BlockSpec((4 * H, K), lambda i, q: (part, 0))],
    )
    return pl.pallas_call(
        partial_kernel,
        grid_spec=grid_spec,
        out_shape=[jax.ShapeDtypeStruct((H, F), bf16)] * 3
        + [jax.ShapeDtypeStruct((H, TILE), bf16)] * steps
        + [jax.ShapeDtypeStruct((4 * S, K), bf16)],
        input_output_aliases={6: 3 + steps} if earlier else {},
        compiler_params=PARAMS,
        cost_estimate=cost(TF),
        name="block_partials",
    )(q, *blocks, weight, *earlier, *wait)


def gelu_kernel(part, xl_ref, own_ref, core_ref, far_ref, cot_ref, *refs):
    act_ref, *outs = refs[-(2 + N + part * N):]
    halves, grad_ref, pieces = outs[:N], outs[N], outs[N + 1:]
    xl = xl_ref[0]
    for chunk, (start, units) in enumerate(CHUNKS):
        size = units * LANE
        base = place(chunk)
        for d in range(DEPTH):
            at = slice(d * UNITS * LANE + start * LANE, d * UNITS * LANE + start * LANE + size)
            pre = own_ref[:, at].astype(f32) + core_ref[:, at].astype(f32) + far_ref[:, at].astype(f32)
            inner = gelu_coef * (pre + 0.044715 * pre * pre * pre)
            tangent = jnp.tanh(inner)
            act_ref[:, at] = (0.5 * pre * (1.0 + tangent)).astype(bf16)
            slope = 0.5 * (1.0 + tangent) + 0.5 * pre * (1.0 - tangent * tangent) * gelu_coef * (
                1.0 + 3.0 * 0.044715 * pre * pre
            )
            grad = (cot_ref[:, at].astype(f32) * slope).astype(bf16)
            grad_ref[:, base + d * size:base + (d + 1) * size] = grad
            if part:
                pieces[chunk][:, d * size:(d + 1) * size] = grad
            if d % 2:
                to = d // 2 * size
                halves[chunk][:, to:to + size] = jnp.where(xl == 0, grad, even)
            else:
                even = grad


def gelu_pair(xl, own, core, far, cot, part, earlier, wait):
    rows = 64
    steps = H // rows
    whole = lambda w: pl.BlockSpec((rows, w), lambda i, x: (i + part * steps, 0))
    local = lambda w: pl.BlockSpec((rows, w), lambda i, x: (i, 0))
    widths = [width(chunk) for chunk in range(N)]
    extra = widths if part else []
    grid_spec = pltpu.PrefetchScalarGridSpec(
        num_scalar_prefetch=1,
        grid=(steps,),
        in_specs=[local(F)] * 3 + [whole(F)] + [ANY] * (len(earlier) + len(wait)),
        out_specs=[whole(F)] + [whole(w // 2) for w in widths] + [local(w) for w in [F] + extra],
    )
    return pl.pallas_call(
        lambda *refs: gelu_kernel(part, *refs),
        grid_spec=grid_spec,
        out_shape=[jax.ShapeDtypeStruct((S, F), bf16)]
        + [jax.ShapeDtypeStruct((S, w // 2), bf16) for w in widths]
        + [jax.ShapeDtypeStruct((H, w), bf16) for w in [F] + extra],
        input_output_aliases={5 + i: i for i in range(len(earlier))},
        compiler_params=PARAMS,
        cost_estimate=cost(TG),
        name="gelu_pair",
    )(xl, own, core, far, cot, *earlier, *wait)


def weight_kernel(size, masks, halves, ids_ref, tk_ref, tx_ref, *refs):
    count = max(1, len(masks))
    groups = [refs[12 * n:12 * (n + 1)] for n in range(count)]
    outs, pg = refs[-(1 + count * (1 + halves)):-1], refs[-1]

    @pl.when(pl.program_id(0) == 0)
    def _():
        xl, r = ids_ref[0], ids_ref[1]
        for n in range(len(masks) or 4):
            cols = slice(n * size, (n + 1) * size)
            own = near = slice(None)
            if not masks:
                own = pl.ds(pl.multiple_of((2 * n + xl) * size, size), size)
                near = cols
            group = groups[n if masks else 0]
            for k in range(4):
                for part in range(2):
                    row = (4 * part + k) * H
                    pg[row:row + H, cols] = group[4 * part + k][:, own]
                slot = pl.multiple_of(4 * S + jnp.bitwise_xor(r, k) * S, S)
                pg[pl.ds(slot, S), cols] = group[8 + k][:, near]

    tokens = jnp.concatenate([tk_ref[...], tx_ref[...]], axis=0)
    total = lax.dot_general(tokens, pg[...], (((0,), (0,)), ((), ())), preferred_element_type=f32).astype(bf16)
    if halves:
        for n, out_ref in enumerate(outs):

            @pl.when(pl.program_id(0) == n)
            def _():
                out_ref[...] = total

    else:
        for n in range(len(masks) or 4):
            piece = total[:, n * size:(n + 1) * size]
            if masks:
                outs[n][...] = piece
            else:
                outs[0][n] = piece


def weight_part(ids, tk, tx, first, second, other, chunk, masks, halves, wait):
    w = width(chunk)
    size = CHUNKS[chunk][1] * LANE
    rows = K // 2 if len(masks) == 1 else 512
    specs = []
    for m in masks:
        for array in (*first, *second):
            at = place(chunk) // size if array.shape[1] == F else 0
            specs.append(
                pl.BlockSpec((H, size), lambda i, x, at=at, m=m: (0, at + 2 * jnp.bitwise_xor(x[2], m) + x[0]))
            )
        specs += [pl.BlockSpec((S, size), lambda i, x, m=m: (0, jnp.bitwise_xor(x[2], m)))] * 4
    if not masks:
        for array in (*first, *second):
            at = place(chunk) // w if array.shape[1] == F else 0
            specs.append(pl.BlockSpec((H, w), lambda i, x, at=at: (0, at)))
        specs += [pl.BlockSpec((S, w // 2), lambda i, x: (0, 0))] * 4
    if halves:
        out_specs = [pl.BlockSpec((rows, size), lambda i, x: (0, 0))] * 2
        out_shape = [jax.ShapeDtypeStruct((rows, size), bf16)] * 2
    elif masks:
        out_specs = [pl.BlockSpec((rows, size), lambda i, x: (i, 0))] * len(masks)
        out_shape = [jax.ShapeDtypeStruct((K, size), bf16)] * len(masks)
    else:
        out_specs = pl.BlockSpec((4, rows, size), lambda i, x: (0, i, 0))
        out_shape = jax.ShapeDtypeStruct((4, K, size), bf16)
    grid_spec = pltpu.PrefetchScalarGridSpec(
        num_scalar_prefetch=1,
        grid=(K // rows,),
        in_specs=[pl.BlockSpec((4 * S, rows), lambda i, x: (0, i))] * 2 + specs + [ANY] * len(wait),
        out_specs=out_specs,
        scratch_shapes=[pltpu.VMEM((8 * S, size * (len(masks) or 4)), bf16)],
    )
    return pl.pallas_call(
        lambda *refs: weight_kernel(size, masks, halves, *refs),
        grid_spec=grid_spec,
        out_shape=out_shape,
        compiler_params=PARAMS,
        cost_estimate=cost(TK),
        name="weight_part",
    )(ids, tk, tx, *([*first, *second, *other] * max(1, len(masks))), *wait)


def relay_kernel(a_ref, b_ref, last_ref, first_ref, a_out, b_out):
    a_out[...] = (a_ref[...].astype(f32) + last_ref[...].astype(f32)).astype(bf16)
    b_out[...] = (b_ref[...].astype(f32) + first_ref[...].astype(f32)).astype(bf16)


def relay(a, b, last, first):
    rows, columns = last.shape[0] // 2, last.shape[1]
    top = pl.BlockSpec((rows, columns), lambda i: (i, 0))
    bottom = pl.BlockSpec((rows, columns), lambda i: (i + 2, 0))
    return pl.pallas_call(
        relay_kernel,
        grid=(2,),
        in_specs=[bottom, top, top, top],
        out_specs=[bottom, top],
        out_shape=[jax.ShapeDtypeStruct(a.shape, bf16)] * 2,
        input_output_aliases={0: 0, 1: 1},
        compiler_params=PARAMS,
        cost_estimate=cost(TK),
        name="relay",
    )(a, b, last, first)


def input_kernel(counts, r_ref, *refs):
    total = sum(counts)
    w_ref, out_ref = refs[total], refs[-1]
    w = jnp.concatenate(
        [
            w_ref[:, (d * UNITS + start) * LANE:(d * UNITS + start + units) * LANE]
            for start, units in (CHUNKS[chunk] for chunk in LAID)
            for d in range(DEPTH)
        ],
        axis=1,
    )
    rows = []
    for count in counts:
        rows.append(jnp.concatenate([ref[...] for ref in refs[:count]], axis=1))
        refs = refs[count:]
    lhs = jnp.concatenate(rows, axis=0)
    total = lax.dot_general(lhs, w, (((1,), (1,)), ((), ())), preferred_element_type=f32).astype(bf16)
    for k in range(4):
        out_ref[jnp.bitwise_xor(r_ref[1], k)] = total[k * H:(k + 1) * H, :]


def input_part(ids, grads, weight, part, earlier, wait):
    tile = 512
    arrays = [array for block in grads for array in block]
    counts = [len(block) for block in grads]
    grid_spec = pltpu.PrefetchScalarGridSpec(
        num_scalar_prefetch=1,
        grid=(K // tile,),
        in_specs=[pl.BlockSpec(array.shape, lambda i, q: (0, 0)) for array in arrays]
        + [pl.BlockSpec((tile, F), lambda i, q: (i, 0))]
        + [ANY] * (len(earlier) + len(wait)),
        out_specs=pl.BlockSpec((4, H, tile), lambda i, q: (0, part, i)),
    )
    return pl.pallas_call(
        lambda *refs: input_kernel(counts, *refs),
        grid_spec=grid_spec,
        out_shape=jax.ShapeDtypeStruct((4, S, K), bf16),
        input_output_aliases={len(arrays) + 2: 0} if earlier else {},
        compiler_params=PARAMS,
        cost_estimate=cost(TK),
        name="input_part",
    )(ids, *arrays, weight, *earlier, *wait)


def join_kernel(first_ref, *refs):
    size = first_ref.shape[1]
    total = refs[0][...].astype(f32)
    for ref in refs[1:-1]:
        total += ref[...].astype(f32)
    refs[-1][:, :size] = first_ref[...]
    refs[-1][:, size:] = total.astype(bf16)


def join(first, pieces, wait):
    rows = 768
    block = lambda size: pl.BlockSpec((rows, size), lambda i: (i, 0))
    sizes = [first.shape[1], pieces[0].shape[1]]
    return pl.pallas_call(
        lambda *refs: join_kernel(*refs[:1 + len(pieces)], refs[-1]),
        grid=(K // rows,),
        in_specs=[block(sizes[0])] + [block(sizes[1])] * len(pieces) + [ANY],
        out_specs=block(sum(sizes)),
        out_shape=jax.ShapeDtypeStruct((K, sum(sizes)), bf16),
        compiler_params=PARAMS,
        cost_estimate=cost(TK),
        name="join",
    )(first, *pieces, wait)


def add_kernel(a_ref, *refs):
    out_ref = refs[-1]
    for n in range(F // TILE):
        at = slice(n * TILE, (n + 1) * TILE)
        out_ref[:, at] = (a_ref[:, at].astype(f32) + refs[n][...].astype(f32)).astype(bf16)


def add(a, pieces, wait):
    block = pl.BlockSpec((H, F), lambda i: (0, 0))
    return pl.pallas_call(
        add_kernel,
        grid=(1,),
        in_specs=[block] + [pl.BlockSpec((H, TILE), lambda i: (0, 0))] * len(pieces) + [ANY],
        out_specs=block,
        out_shape=jax.ShapeDtypeStruct(a.shape, bf16),
        compiler_params=PARAMS,
        cost_estimate=cost(1),
        name="add",
    )(a, *pieces, wait)


def fold_kernel(in_ref, out_ref):
    total = in_ref[0].astype(f32)
    for n in range(1, in_ref.shape[0]):
        total += in_ref[n].astype(f32)
    out_ref[...] = total.astype(bf16)


def fold(pieces):
    count, rows, columns = pieces.shape
    tile = rows // 2
    return pl.pallas_call(
        fold_kernel,
        grid=(2,),
        in_specs=[pl.BlockSpec((count, tile, columns), lambda i: (0, i, 0))],
        out_specs=pl.BlockSpec((tile, columns), lambda i: (i, 0)),
        out_shape=jax.ShapeDtypeStruct((rows, columns), bf16),
        compiler_params=PARAMS,
        cost_estimate=cost(TK),
        name="fold",
    )(pieces)


def swap(value, axis, mask):
    n = lax.axis_size(axis)
    return lax.ppermute(value, axis, [(i, i ^ mask) for i in range(n)])


def shards(tokens, weight, cotangent):
    xh, core, y, xl, z = (lax.axis_index(a) for a in ("xh", "core", "y", "xl", "z"))
    r = 2 * xh + core
    q = jnp.bitwise_xor(r, y).astype(jnp.int32).reshape(1)
    ids = jnp.stack([xl, r, z]).astype(jnp.int32)

    partner = swap(tokens, "xl", 1)
    tx = lax.all_gather(partner, "y", axis=0, tiled=True)
    mine = [tokens[:H], tokens[H:]]
    around = [[swap(half, "y", m) for m in (1, 2, 3)] for half in mine]
    around[1] = after(around[1], tokens, TE)

    p0, p1, p2, *p3, tk = block_partials(q, [mine[0], *around[0]], weight, 0, (), ())
    total = add(p2, [swap(v, "core", 1) for v in p3], around[1][0])
    (far,) = after([swap(total, "xh", 1)], total, T3)
    terms = [p0, swap(p1, "core", 1), far]
    p0, p1, p2, *p3, tk = block_partials(q, [mine[1], *around[1]], weight, 1, (tk,), (total, partner))
    total = add(p2, [swap(v, "core", 1) for v in p3], total)
    *shared, first = gelu_pair(ids, *terms, cotangent, 0, (), ())
    terms = [p0, swap(p1, "core", 1), swap(total, "xh", 1)]
    first_far = swap(first, "xh", 1)
    activation, *halves, second, second_a, second_b = gelu_pair(ids, *terms, cotangent, 1, shared, ())
    far = [swap(value, "xh", 1) for value in (second_a, second_b)]
    near = [swap(half, "xl", 1) for half in halves]
    cross = [lax.ppermute(half, ("xh", "xl"), [(i, 3 - i) for i in range(4)]) for half in halves]

    def pairs(values, wait, micros=300):
        return [(value, swap(value, "core", 1)) for value in after(values, wait, micros)]

    (first, first_core), first_far, (second, second_core) = pairs([first, first_far, second], halves[0])
    first = [first, first_core, *first_far]
    dx = input_part(ids, [[value] for value in first], weight, 0, (), (second_core, tx))
    far[0], near[0], cross[0] = pairs([far[0], near[0], cross[0]], dx)
    own = [second, second_core]
    dw0 = weight_part(ids, tk, tx, first, [*own, *far[0]], [*near[0], *cross[0]], 0, (), False, ())
    (far[1],) = pairs([far[1]], dw0)
    blocks = [[value] for value in own] + [[far[chunk][c] for chunk in LAID] for c in range(2)]
    dx = input_part(ids, blocks, weight, 1, (dx,), ())
    near[1], cross[1] = pairs([near[1], cross[1]], dx, T4)
    dw0 = lax.psum_scatter(dw0, "z", scatter_dimension=0, tiled=True)[0]
    last = [first, [*own, *far[1]], [*near[1], *cross[1]], 1]
    top, bottom = weight_part(ids, tk, tx, *last, (2,), True, ())
    to_right, to_left = swap(top, "z", 1), swap(bottom, "z", 3)
    one, three = weight_part(ids, tk, tx, *last, (1, 3), False, (top, dw0))
    one, three = relay(one, three, to_left, to_right)
    (mine,) = weight_part(ids, tk, tx, *last, (0,), False, (one,))

    (dx,) = after([lax.all_to_all(dx, "y", 0, 0, tiled=True)], total, T5)
    input_grad = fold(dx)
    weight_grad = join(dw0, [mine, swap(one, "z", 1), swap(three, "z", 3)], input_grad)
    return activation, input_grad, weight_grad


def solution(mesh):
    split = Mesh(mesh.devices.reshape(2, 2, 4, 4, 2), ("xh", "core", "y", "z", "xl"))
    hidden = P(("z", "xl", "xh", "core"), "y")
    tokens = P(("z", "xl", "y"), ("xh", "core"))
    return jax.shard_map(
        shards,
        mesh=split,
        in_specs=(tokens, P(("xh", "core"), "y"), hidden),
        out_specs=(hidden, tokens, P(("xh", "core"), ("y", "z", "xl"))),
        check_vma=False,
    )
```

```python
import jax
import jax.numpy as jnp
from jax import lax
from jax.experimental import pallas as pl
from jax.experimental.pallas import tpu as pltpu
from jax.sharding import Mesh
from jax.sharding import PartitionSpec as P

K = 1536
F = 3072
S = 256
H = 128
TILE = 1024
DEPTH = 8
LANE = 128
UNITS = F // (DEPTH * LANE)
CHUNKS = ((0, 1), (1, 2))
N = len(CHUNKS)
LAID = (1, 0)
gelu_coef = 0.7978845608028654
bf16 = jnp.bfloat16
f32 = jnp.float32
MIB = 1 << 20
TF, TG, TK, TE, T3, T4, T5 = 0.01, 30, 0.5, 300, 2, 300, 300
ANY = pl.BlockSpec(memory_space=pl.ANY)
PARAMS = pltpu.CompilerParams(vmem_limit_bytes=64 * MIB)


def cost(micros):
    return pl.CostEstimate(flops=int(micros * 1.15e9), bytes_accessed=int(micros * 3.6e6), transcendentals=0)


def width(chunk):
    return DEPTH * CHUNKS[chunk][1] * LANE


def place(chunk):
    return sum(width(other) for other in LAID[:LAID.index(chunk)])


def after_kernel(*refs):
    pass


def after(values, other, micros=300):
    return pl.pallas_call(
        after_kernel,
        in_specs=[ANY] * (len(values) + 1),
        out_specs=[ANY] * len(values),
        out_shape=[jax.ShapeDtypeStruct(value.shape, value.dtype) for value in values],
        input_output_aliases={n: n for n in range(len(values))},
        cost_estimate=cost(micros),
        name="after",
    )(*values, other)


def partial_kernel(q_ref, b0, b1, b2, b3, w_ref, *refs):
    p0_ref, p1_ref, p2_ref, *p3_refs, tk_ref = refs[-(4 + F // TILE):]

    @pl.when(pl.program_id(0) == 0)
    def _():
        q = q_ref[0]
        for m, block in enumerate((b0, b1, b2, b3)):
            slot = pl.multiple_of(jnp.bitwise_xor(q, m) * H, H)
            tk_ref[pl.ds(slot, H), :] = block[...]

    term = jnp.dot(tk_ref[...], w_ref[...], preferred_element_type=f32).astype(bf16)
    for k, ref in enumerate((p0_ref, p1_ref, p2_ref)):
        ref[...] = term[k * H:(k + 1) * H, :]
    for n, ref in enumerate(p3_refs):

        @pl.when(pl.program_id(0) == n)
        def _():
            ref[...] = term[3 * H:, :]


def block_partials(q, blocks, weight, part, earlier, wait):
    steps = F // TILE
    rows = [pl.BlockSpec((H, K), lambda i, q, at=part if block.shape[0] == S else 0: (at, 0)) for block in blocks]
    grid_spec = pltpu.PrefetchScalarGridSpec(
        num_scalar_prefetch=1,
        grid=(steps,),
        in_specs=rows + [pl.BlockSpec((K, TILE), lambda i, q: (0, i))] + [ANY] * (len(earlier) + len(wait)),
        out_specs=[pl.BlockSpec((H, TILE), lambda i, q: (0, i))] * 3
        + [pl.BlockSpec((H, TILE), lambda i, q: (0, 0))] * steps
        + [pl.BlockSpec((4 * H, K), lambda i, q: (part, 0))],
    )
    return pl.pallas_call(
        partial_kernel,
        grid_spec=grid_spec,
        out_shape=[jax.ShapeDtypeStruct((H, F), bf16)] * 3
        + [jax.ShapeDtypeStruct((H, TILE), bf16)] * steps
        + [jax.ShapeDtypeStruct((4 * S, K), bf16)],
        input_output_aliases={6: 3 + steps} if earlier else {},
        compiler_params=PARAMS,
        cost_estimate=cost(TF),
        name="block_partials",
    )(q, *blocks, weight, *earlier, *wait)


def gelu_kernel(part, xl_ref, own_ref, core_ref, far_ref, cot_ref, *refs):
    act_ref, *outs = refs[-(2 + N + part * N):]
    halves, grad_ref, pieces = outs[:N], outs[N], outs[N + 1:]
    xl = xl_ref[0]
    for chunk, (start, units) in enumerate(CHUNKS):
        size = units * LANE
        base = place(chunk)
        for d in range(DEPTH):
            at = slice(d * UNITS * LANE + start * LANE, d * UNITS * LANE + start * LANE + size)
            pre = own_ref[:, at].astype(f32) + core_ref[:, at].astype(f32) + far_ref[:, at].astype(f32)
            inner = gelu_coef * (pre + 0.044715 * pre * pre * pre)
            tangent = jnp.tanh(inner)
            act_ref[:, at] = (0.5 * pre * (1.0 + tangent)).astype(bf16)
            slope = 0.5 * (1.0 + tangent) + 0.5 * pre * (1.0 - tangent * tangent) * gelu_coef * (
                1.0 + 3.0 * 0.044715 * pre * pre
            )
            grad = (cot_ref[:, at].astype(f32) * slope).astype(bf16)
            grad_ref[:, base + d * size:base + (d + 1) * size] = grad
            if part:
                pieces[chunk][:, d * size:(d + 1) * size] = grad
            if d % 2:
                to = d // 2 * size
                halves[chunk][:, to:to + size] = jnp.where(xl == 0, grad, even)
            else:
                even = grad


def gelu_pair(xl, own, core, far, cot, part, earlier, wait):
    rows = 64
    steps = H // rows
    whole = lambda w: pl.BlockSpec((rows, w), lambda i, x: (i + part * steps, 0))
    local = lambda w: pl.BlockSpec((rows, w), lambda i, x: (i, 0))
    widths = [width(chunk) for chunk in range(N)]
    extra = widths if part else []
    grid_spec = pltpu.PrefetchScalarGridSpec(
        num_scalar_prefetch=1,
        grid=(steps,),
        in_specs=[local(F)] * 3 + [whole(F)] + [ANY] * (len(earlier) + len(wait)),
        out_specs=[whole(F)] + [whole(w // 2) for w in widths] + [local(w) for w in [F] + extra],
    )
    return pl.pallas_call(
        lambda *refs: gelu_kernel(part, *refs),
        grid_spec=grid_spec,
        out_shape=[jax.ShapeDtypeStruct((S, F), bf16)]
        + [jax.ShapeDtypeStruct((S, w // 2), bf16) for w in widths]
        + [jax.ShapeDtypeStruct((H, w), bf16) for w in [F] + extra],
        input_output_aliases={5 + i: i for i in range(len(earlier))},
        compiler_params=PARAMS,
        cost_estimate=cost(TG),
        name="gelu_pair",
    )(xl, own, core, far, cot, *earlier, *wait)


def weight_kernel(size, masks, halves, ids_ref, tk_ref, tx_ref, *refs):
    count = max(1, len(masks))
    groups = [refs[12 * n:12 * (n + 1)] for n in range(count)]
    outs, pg = refs[-(1 + count * (1 + halves)):-1], refs[-1]

    @pl.when(pl.program_id(0) == 0)
    def _():
        xl, r = ids_ref[0], ids_ref[1]
        for n in range(len(masks) or 4):
            cols = slice(n * size, (n + 1) * size)
            own = near = slice(None)
            if not masks:
                own = pl.ds(pl.multiple_of((2 * n + xl) * size, size), size)
                near = cols
            group = groups[n if masks else 0]
            for k in range(4):
                for part in range(2):
                    row = (4 * part + k) * H
                    pg[row:row + H, cols] = group[4 * part + k][:, own]
                slot = pl.multiple_of(4 * S + jnp.bitwise_xor(r, k) * S, S)
                pg[pl.ds(slot, S), cols] = group[8 + k][:, near]

    tokens = jnp.concatenate([tk_ref[...], tx_ref[...]], axis=0)
    total = lax.dot_general(tokens, pg[...], (((0,), (0,)), ((), ())), preferred_element_type=f32).astype(bf16)
    if halves:
        for n, out_ref in enumerate(outs):

            @pl.when(pl.program_id(0) == n)
            def _():
                out_ref[...] = total

    else:
        for n in range(len(masks) or 4):
            piece = total[:, n * size:(n + 1) * size]
            if masks:
                outs[n][...] = piece
            else:
                outs[0][n] = piece


def weight_part(ids, tk, tx, first, second, other, chunk, masks, halves, wait):
    w = width(chunk)
    size = CHUNKS[chunk][1] * LANE
    rows = K // 2
    specs = []
    for m in masks:
        for array in (*first, *second):
            at = place(chunk) // size if array.shape[1] == F else 0
            specs.append(
                pl.BlockSpec((H, size), lambda i, x, at=at, m=m: (0, at + 2 * jnp.bitwise_xor(x[2], m) + x[0]))
            )
        specs += [pl.BlockSpec((S, size), lambda i, x, m=m: (0, jnp.bitwise_xor(x[2], m)))] * 4
    if not masks:
        for array in (*first, *second):
            at = place(chunk) // w if array.shape[1] == F else 0
            specs.append(pl.BlockSpec((H, w), lambda i, x, at=at: (0, at)))
        specs += [pl.BlockSpec((S, w // 2), lambda i, x: (0, 0))] * 4
    if halves:
        out_specs = [pl.BlockSpec((rows, size), lambda i, x: (0, 0))] * 2
        out_shape = [jax.ShapeDtypeStruct((rows, size), bf16)] * 2
    elif masks:
        out_specs = [pl.BlockSpec((rows, size), lambda i, x: (i, 0))] * len(masks)
        out_shape = [jax.ShapeDtypeStruct((K, size), bf16)] * len(masks)
    else:
        out_specs = pl.BlockSpec((4, rows, size), lambda i, x: (0, i, 0))
        out_shape = jax.ShapeDtypeStruct((4, K, size), bf16)
    grid_spec = pltpu.PrefetchScalarGridSpec(
        num_scalar_prefetch=1,
        grid=(K // rows,),
        in_specs=[pl.BlockSpec((4 * S, rows), lambda i, x: (0, i))] * 2 + specs + [ANY] * len(wait),
        out_specs=out_specs,
        scratch_shapes=[pltpu.VMEM((8 * S, size * (len(masks) or 4)), bf16)],
    )
    return pl.pallas_call(
        lambda *refs: weight_kernel(size, masks, halves, *refs),
        grid_spec=grid_spec,
        out_shape=out_shape,
        compiler_params=PARAMS,
        cost_estimate=cost(TK),
        name="weight_part",
    )(ids, tk, tx, *([*first, *second, *other] * max(1, len(masks))), *wait)


def relay_kernel(a_ref, b_ref, last_ref, first_ref, a_out, b_out):
    a_out[...] = (a_ref[...].astype(f32) + last_ref[...].astype(f32)).astype(bf16)
    b_out[...] = (b_ref[...].astype(f32) + first_ref[...].astype(f32)).astype(bf16)


def relay(a, b, last, first):
    rows, columns = last.shape[0] // 2, last.shape[1]
    top = pl.BlockSpec((rows, columns), lambda i: (i, 0))
    bottom = pl.BlockSpec((rows, columns), lambda i: (i + 2, 0))
    return pl.pallas_call(
        relay_kernel,
        grid=(2,),
        in_specs=[bottom, top, top, top],
        out_specs=[bottom, top],
        out_shape=[jax.ShapeDtypeStruct(a.shape, bf16)] * 2,
        input_output_aliases={0: 0, 1: 1},
        compiler_params=PARAMS,
        cost_estimate=cost(TK),
        name="relay",
    )(a, b, last, first)


def input_kernel(counts, r_ref, *refs):
    total = sum(counts)
    w_ref, out_ref = refs[total], refs[-1]
    w = jnp.concatenate(
        [
            w_ref[:, (d * UNITS + start) * LANE:(d * UNITS + start + units) * LANE]
            for start, units in (CHUNKS[chunk] for chunk in LAID)
            for d in range(DEPTH)
        ],
        axis=1,
    )
    rows = []
    for count in counts:
        rows.append(jnp.concatenate([ref[...] for ref in refs[:count]], axis=1))
        refs = refs[count:]
    lhs = jnp.concatenate(rows, axis=0)
    total = lax.dot_general(lhs, w, (((1,), (1,)), ((), ())), preferred_element_type=f32).astype(bf16)
    for k in range(4):
        out_ref[jnp.bitwise_xor(r_ref[1], k)] = total[k * H:(k + 1) * H, :]


def input_part(ids, grads, weight, part, earlier, wait):
    tile = 512
    arrays = [array for block in grads for array in block]
    counts = [len(block) for block in grads]
    grid_spec = pltpu.PrefetchScalarGridSpec(
        num_scalar_prefetch=1,
        grid=(K // tile,),
        in_specs=[pl.BlockSpec(array.shape, lambda i, q: (0, 0)) for array in arrays]
        + [pl.BlockSpec((tile, F), lambda i, q: (i, 0))]
        + [ANY] * (len(earlier) + len(wait)),
        out_specs=pl.BlockSpec((4, H, tile), lambda i, q: (0, part, i)),
    )
    return pl.pallas_call(
        lambda *refs: input_kernel(counts, *refs),
        grid_spec=grid_spec,
        out_shape=jax.ShapeDtypeStruct((4, S, K), bf16),
        input_output_aliases={len(arrays) + 2: 0} if earlier else {},
        compiler_params=PARAMS,
        cost_estimate=cost(TK),
        name="input_part",
    )(ids, *arrays, weight, *earlier, *wait)


def join_kernel(first_ref, *refs):
    size = first_ref.shape[1]
    total = refs[0][...].astype(f32)
    for ref in refs[1:-1]:
        total += ref[...].astype(f32)
    refs[-1][:, :size] = first_ref[...]
    refs[-1][:, size:] = total.astype(bf16)


def join(first, pieces, wait):
    rows = 768
    block = lambda size: pl.BlockSpec((rows, size), lambda i: (i, 0))
    sizes = [first.shape[1], pieces[0].shape[1]]
    return pl.pallas_call(
        lambda *refs: join_kernel(*refs[:1 + len(pieces)], refs[-1]),
        grid=(K // rows,),
        in_specs=[block(sizes[0])] + [block(sizes[1])] * len(pieces) + [ANY],
        out_specs=block(sum(sizes)),
        out_shape=jax.ShapeDtypeStruct((K, sum(sizes)), bf16),
        compiler_params=PARAMS,
        cost_estimate=cost(TK),
        name="join",
    )(first, *pieces, wait)


def add_kernel(a_ref, *refs):
    out_ref = refs[-1]
    for n in range(F // TILE):
        at = slice(n * TILE, (n + 1) * TILE)
        out_ref[:, at] = (a_ref[:, at].astype(f32) + refs[n][...].astype(f32)).astype(bf16)


def add(a, pieces, wait):
    block = pl.BlockSpec((H, F), lambda i: (0, 0))
    return pl.pallas_call(
        add_kernel,
        grid=(1,),
        in_specs=[block] + [pl.BlockSpec((H, TILE), lambda i: (0, 0))] * len(pieces) + [ANY],
        out_specs=block,
        out_shape=jax.ShapeDtypeStruct(a.shape, bf16),
        compiler_params=PARAMS,
        cost_estimate=cost(1),
        name="add",
    )(a, *pieces, wait)


def fold_kernel(in_ref, out_ref):
    total = in_ref[0].astype(f32)
    for n in range(1, in_ref.shape[0]):
        total += in_ref[n].astype(f32)
    out_ref[...] = total.astype(bf16)


def fold(pieces):
    count, rows, columns = pieces.shape
    tile = rows // 2
    return pl.pallas_call(
        fold_kernel,
        grid=(2,),
        in_specs=[pl.BlockSpec((count, tile, columns), lambda i: (0, i, 0))],
        out_specs=pl.BlockSpec((tile, columns), lambda i: (i, 0)),
        out_shape=jax.ShapeDtypeStruct((rows, columns), bf16),
        compiler_params=PARAMS,
        cost_estimate=cost(TK),
        name="fold",
    )(pieces)


def swap(value, axis, mask):
    n = lax.axis_size(axis)
    return lax.ppermute(value, axis, [(i, i ^ mask) for i in range(n)])


def shards(tokens, weight, cotangent):
    xh, core, y, xl, z = (lax.axis_index(a) for a in ("xh", "core", "y", "xl", "z"))
    r = 2 * xh + core
    q = jnp.bitwise_xor(r, y).astype(jnp.int32).reshape(1)
    ids = jnp.stack([xl, r, z]).astype(jnp.int32)

    partner = swap(tokens, "xl", 1)
    tx = lax.all_gather(partner, "y", axis=0, tiled=True)
    mine = [tokens[:H], tokens[H:]]
    around = [[swap(half, "y", m) for m in (1, 2, 3)] for half in mine]
    around[1] = after(around[1], tokens, TE)

    p0, p1, p2, *p3, tk = block_partials(q, [mine[0], *around[0]], weight, 0, (), ())
    total = add(p2, [swap(v, "core", 1) for v in p3], around[1][0])
    (far,) = after([swap(total, "xh", 1)], total, T3)
    terms = [p0, swap(p1, "core", 1), far]
    p0, p1, p2, *p3, tk = block_partials(q, [mine[1], *around[1]], weight, 1, (tk,), (total, partner))
    total = add(p2, [swap(v, "core", 1) for v in p3], total)
    *shared, first = gelu_pair(ids, *terms, cotangent, 0, (), ())
    terms = [p0, swap(p1, "core", 1), swap(total, "xh", 1)]
    first_far = swap(first, "xh", 1)
    activation, *halves, second, second_a, second_b = gelu_pair(ids, *terms, cotangent, 1, shared, ())
    far = [swap(value, "xh", 1) for value in (second_a, second_b)]
    near = [swap(half, "xl", 1) for half in halves]
    cross = [lax.ppermute(half, ("xh", "xl"), [(i, 3 - i) for i in range(4)]) for half in halves]

    def pairs(values, wait, micros=300):
        return [(value, swap(value, "core", 1)) for value in after(values, wait, micros)]

    (first, first_core), first_far, (second, second_core) = pairs([first, first_far, second], halves[0])
    first = [first, first_core, *first_far]
    dx = input_part(ids, [[value] for value in first], weight, 0, (), (second_core, tx))
    far[0], near[0], cross[0] = pairs([far[0], near[0], cross[0]], dx)
    own = [second, second_core]
    dw0 = weight_part(ids, tk, tx, first, [*own, *far[0]], [*near[0], *cross[0]], 0, (), False, ())
    (far[1],) = pairs([far[1]], dw0)
    blocks = [[value] for value in own] + [[far[chunk][c] for chunk in LAID] for c in range(2)]
    dx = input_part(ids, blocks, weight, 1, (dx,), ())
    near[1], cross[1] = pairs([near[1], cross[1]], dx, T4)
    dw0 = lax.psum_scatter(dw0, "z", scatter_dimension=0, tiled=True)[0]
    last = [first, [*own, *far[1]], [*near[1], *cross[1]], 1]
    top, bottom = weight_part(ids, tk, tx, *last, (2,), True, ())
    to_right, to_left = swap(top, "z", 1), swap(bottom, "z", 3)
    one, three = weight_part(ids, tk, tx, *last, (1, 3), False, (top, dw0))
    one, three = relay(one, three, to_left, to_right)
    (mine,) = weight_part(ids, tk, tx, *last, (0,), False, (one,))

    (dx,) = after([lax.all_to_all(dx, "y", 0, 0, tiled=True)], total, T5)
    input_grad = fold(dx)
    weight_grad = join(dw0, [mine, swap(one, "z", 1), swap(three, "z", 3)], input_grad)
    return activation, input_grad, weight_grad


def solution(mesh):
    split = Mesh(mesh.devices.reshape(2, 2, 4, 4, 2), ("xh", "core", "y", "z", "xl"))
    hidden = P(("z", "xl", "xh", "core"), "y")
    tokens = P(("z", "xl", "y"), ("xh", "core"))
    return jax.shard_map(
        shards,
        mesh=split,
        in_specs=(tokens, P(("xh", "core"), "y"), hidden),
        out_specs=(hidden, tokens, P(("xh", "core"), ("y", "z", "xl"))),
        check_vma=False,
    )
```
